32 devices in a mesh: rows: 4 (over x, core), cols: 8 (over z, y).
Axes of the slice: x: 2, y: 2, z: 4, core: 2. Of those that a mesh axis runs over, the one named last changes fastest.
Arguments:
- kernels: float32 [10240, 128, 128], P(('rows', 'cols')), may hold values from -0.1875 to 0.1875
- pick_index: int32 [10240], P(('rows', 'cols')), may hold values from 0 to 127
- cell_index: int32 [10240], P(('rows', 'cols')), may hold values from 0 to 511
- counts: int32 [4, 8], P('rows', 'cols'), may hold values from 80 to 320, as said below
- data: float32 [128, 512], P('cols', 'rows'), may hold values from -6 to 6
Outputs:
- model: float32 [512, 1024], P('rows', 'cols')
- search: float32 [512, 1024], P('rows', 'cols')
The draws below stay inside these ranges and needn't reach their ends.
Inputs may be any that keep to these rules, and one draw needn't show every extreme that they name: `counts`: every device has at least 80 live tiles, and some device has all 320 slots live.
All inputs are finite; a program needn't handle non-finite values.
Results may differ from the reference program's by a relative error of at most 0.0003.
Values sent between devices are 32-bit elements; how exact they have to be, the bound alone decides.
No kernel may reach another device: no remote copies, remote signals or barrier semaphores. Data moves between devices by JAX's collectives and lax.ppermute only.
A program may use at most 64 MiB of HBM per device.

```python
import math
import jax
import jax.numpy as jnp
import numpy as np
from jax import lax

B = 128
KMAX = 320
PBLK = 128
CBLK = 512
ITERS = 2
N_ROWS = 4
N_COLS = 8


def draw_counts(key, part):
    key = jax.random.fold_in(key, 7)
    values = jax.random.randint(key, (N_ROWS * N_COLS,), KMAX // 4, KMAX + 1, dtype=jnp.int32)
    filled = jax.random.randint(jax.random.fold_in(key, 1), (), 0, N_ROWS * N_COLS, dtype=jnp.int32)
    values = values.at[filled].set(KMAX)
    return values.reshape(N_ROWS, N_COLS)


def plant(values, key, low, largest):
    longest = values.shape.index(max(values.shape))
    spots = []
    for shift in (0, 1):
        where = [jax.random.randint(jax.random.fold_in(key, axis), (), 0, length) for axis, length in enumerate(values.shape)]
        where[longest] = (where[longest] + shift) % values.shape[longest]
        spots.append(tuple(where))
    return values.at[spots[0]].set(low).at[spots[1]].set(largest)


def block_scale(key, shape, pieces, least, largest):
    gain = 1.0
    for position, blocks in pieces:
        draws = jax.random.uniform(jax.random.fold_in(jax.random.fold_in(key, 6), position), (blocks,), jnp.float32, least / len(pieces), largest / len(pieces))
        gain = gain * jnp.repeat(jnp.exp(draws), shape[position] // blocks).reshape((-1,) + (1,) * (len(shape) - 1 - position))
    return gain


def rank_bounds(count, slope):
    loads = [(1 << 20) // math.isqrt(standing ** slope) + 1 for standing in range(1, count + 1)]
    deviation = 1 + sum(loads) // (1 << 30)
    return np.cumsum(np.array([max(1, weight // deviation) for weight in loads]))


def skewed_ids(key, shape, amount, lean):
    grid = rank_bounds(amount, lean)
    ticket = jax.random.randint(jax.random.fold_in(key, 1), shape, 0, int(grid[amount - 1]))
    rank = jnp.searchsorted(jnp.asarray(grid, jnp.int32), ticket, side="right")
    return jax.random.permutation(jax.random.fold_in(key, 2), amount)[rank].astype(jnp.int32)


def gaussian(rng, dims, width, bound, shards=(), kind=jnp.bfloat16):
    level = block_scale(rng, dims, shards, -0.22, 0.18) if shards else 1.0
    drawn = jax.random.normal(rng, dims, jnp.float32) * width * level
    return jnp.minimum(jnp.maximum(drawn, -bound), bound).astype(kind)


def setup_inputs(seed: int = 0) -> dict:
    splits = jax.random.split(jax.random.key(seed), 6)
    return {
        "kernels": gaussian(splits[0], (N_ROWS * N_COLS * KMAX, B, B), (B * 8) ** -0.5, 0.1875, ((0, 32),), jnp.float32),
        "pick_index": plant(jax.random.randint(splits[1], (N_ROWS * N_COLS * KMAX,), 0, PBLK), jax.random.fold_in(splits[1], 1), 0, PBLK - 1).astype(jnp.int32),
        "cell_index": plant(skewed_ids(splits[2], (N_ROWS * N_COLS * KMAX,), CBLK, 2), jax.random.fold_in(splits[2], 3), 0, CBLK - 1).astype(jnp.int32),
        "counts": draw_counts(jax.random.fold_in(splits[5], 71), 0),
        "data": gaussian(splits[4], (PBLK, N_ROWS * B), 1.0, 6.0, ((0, 8), (1, 4)), jnp.float32),
    }


def reference(kernels, pick_index, cell_index, counts, data):
    highest = lax.Precision.HIGHEST
    devcount = N_ROWS * N_COLS
    tiles = kernels.reshape(devcount, KMAX, B, B)
    picks = pick_index.reshape(devcount, KMAX)
    cells = cell_index.reshape(devcount, KMAX)
    livecount = counts.reshape(devcount)
    row_ids = jnp.arange(devcount, dtype=jnp.int32) // N_COLS
    col_ids = jnp.arange(devcount, dtype=jnp.int32) % N_COLS

    def forward(vector):
        cube = vector.reshape(CBLK, N_COLS, B)

        def single(items):
            tile, pick, cell, count, row_id, col_id = items
            live = (jnp.arange(KMAX, dtype=jnp.int32) < count).astype(jnp.float32)
            blocks = cube[cell, col_id]
            product = jnp.einsum('kij,kj->ki', tile, blocks, precision=highest) * live[:, None]
            return jnp.zeros((PBLK, B), jnp.float32).at[pick].add(product)
        parts = lax.map(single, (tiles, picks, cells, livecount, row_ids, col_ids))
        summed = parts.reshape(N_ROWS, N_COLS, PBLK, B).sum(axis=1)
        return summed.transpose(1, 0, 2).reshape(PBLK, N_ROWS * B)

    def adjoint(vector):
        cube = vector.reshape(PBLK, N_ROWS, B)

        def single(items):
            tile, pick, cell, count, row_id, col_id = items
            live = (jnp.arange(KMAX, dtype=jnp.int32) < count).astype(jnp.float32)
            blocks = cube[pick, row_id]
            product = jnp.einsum('kij,ki->kj', tile, blocks, precision=highest) * live[:, None]
            return jnp.zeros((CBLK, B), jnp.float32).at[cell].add(product)
        parts = lax.map(single, (tiles, picks, cells, livecount, row_ids, col_ids))
        summed = parts.reshape(N_ROWS, N_COLS, CBLK, B).sum(axis=0)
        return summed.transpose(1, 0, 2).reshape(CBLK, N_COLS * B)
    beta = jnp.sqrt(jnp.sum(data * data))
    upick = data / beta
    vtemp = adjoint(upick)
    alpha = jnp.sqrt(jnp.sum(vtemp * vtemp))
    vcell = vtemp / alpha
    search = vcell
    model = jnp.zeros_like(vcell)
    phibar = beta
    rhobar = alpha
    for step in range(ITERS):
        utemp = forward(vcell) - alpha * upick
        beta = jnp.sqrt(jnp.sum(utemp * utemp))
        upick = utemp / beta
        vtemp = adjoint(upick) - beta * vcell
        alpha = jnp.sqrt(jnp.sum(vtemp * vtemp))
        vcell = vtemp / alpha
        rho = jnp.sqrt(rhobar * rhobar + beta * beta)
        cosine = rhobar / rho
        sine = beta / rho
        theta = sine * alpha
        rhobar = -cosine * alpha
        phi = cosine * phibar
        phibar = sine * phibar
        model = model + phi / rho * search
        search = vcell - theta / rho * search
    return (model, search)
```

```python
import jax
import jax.numpy as jnp
from jax import lax
from jax.sharding import PartitionSpec as P

PBLK = 128
CBLK = 512
ITERS = 2
HIGHEST = lax.Precision.HIGHEST


def pieces_by_offset(parts, axis, size):
    return [parts[0]] + [
        lax.ppermute(parts[d], axis, [(i, (i + d) % size) for i in range(size)])
        for d in range(1, size)
    ]


def gather_blocks(block, axis, size, me):
    got = pieces_by_offset([block] * size, axis, size)
    rows = block.shape[0]
    whole = jnp.concatenate(got[:1] + got[:0:-1], axis=0)
    return jnp.roll(whole, me * rows, axis=0)


def scatter_sum(whole, extra, axis, size, me):
    rows = whole.shape[0] // size
    turned = jnp.roll(whole, -me * rows, axis=0).reshape(size, rows, -1)
    tail = jnp.full((8, whole.shape[1]), extra)
    parts = [jnp.concatenate([turned[d], tail], axis=0) for d in range(size)]
    total = sum(pieces_by_offset(parts, axis, size))
    return total[:rows], total[rows, 0]


def per_device(n_rows, n_cols, kernels, pick_index, cell_index, counts, data):
    slots = kernels.shape[0]
    my_row = lax.axis_index("rows")
    my_col = lax.axis_index("cols")
    live = (lax.iota(jnp.int32, slots) < counts[0, 0]).astype(jnp.float32)
    pick_table = (pick_index[None, :] == lax.iota(jnp.int32, PBLK)[:, None]).astype(
        jnp.float32
    ) * live[None, :]
    cell_table = (cell_index[None, :] == lax.iota(jnp.int32, CBLK)[:, None]).astype(
        jnp.float32
    ) * live[None, :]

    def adjoint(owned):
        group = gather_blocks(owned, "cols", n_cols, my_col)
        product = jnp.einsum("kij,ki->kj", kernels, group[pick_index], precision=HIGHEST)
        whole = jnp.dot(cell_table, product, precision=HIGHEST)
        return scatter_sum(whole, jnp.sum(group * group), "rows", n_rows, my_row)

    def forward(owned):
        group = gather_blocks(owned, "rows", n_rows, my_row)
        product = jnp.einsum("kij,kj->ki", kernels, group[cell_index], precision=HIGHEST)
        whole = jnp.dot(pick_table, product, precision=HIGHEST)
        return scatter_sum(whole, jnp.sum(group * group), "cols", n_cols, my_col)

    product, square = adjoint(data)
    beta = jnp.sqrt(square)
    upick = data
    vcell = product / beta
    phibar = beta
    rhobar = None
    model = jnp.zeros_like(vcell)
    search = None
    for step in range(ITERS):
        product, square = forward(vcell)
        alpha = jnp.sqrt(square)
        if step == 0:
            rhobar = alpha
            search = vcell / alpha
        else:
            theta = sine * alpha
            rhobar = -cosine * alpha
            search = vcell / alpha - theta / rho * search
        upick = product / alpha - alpha * (upick / beta)
        product, square = adjoint(upick)
        beta = jnp.sqrt(square)
        vcell = product / beta - beta * (vcell / alpha)
        rho = jnp.sqrt(rhobar * rhobar + beta * beta)
        cosine = rhobar / rho
        sine = beta / rho
        phi = cosine * phibar
        phibar = sine * phibar
        model = model + phi / rho * search
    square = jnp.full((8, 128), jnp.sum(vcell * vcell))
    square = sum(pieces_by_offset([square] * n_rows, "rows", n_rows))
    square = sum(pieces_by_offset([square] * n_cols, "cols", n_cols))
    alpha = jnp.sqrt(square[0, 0])
    search = vcell / alpha - sine * alpha / rho * search
    return (model, search)


def solution(mesh):
    def run(*args):
        return per_device(mesh.shape["rows"], mesh.shape["cols"], *args)

    return jax.shard_map(
        run,
        mesh=mesh,
        in_specs=(
            P(("rows", "cols"), None, None),
            P(("rows", "cols")),
            P(("rows", "cols")),
            P("rows", "cols"),
            P("cols", "rows"),
        ),
        out_specs=(P("rows", "cols"), P("rows", "cols")),
        check_vma=False,
    )
```

```python
import jax
import jax.numpy as jnp
from jax import lax
from jax.sharding import PartitionSpec as P

PBLK = 128
CBLK = 512
ITERS = 2
HIGHEST = lax.Precision.HIGHEST


def swapped(block, axis, size, bit):
    return lax.ppermute(block, axis, [(i, i ^ bit) for i in range(size)])


def pairwise_sum(block, axis, size):
    bit = 1
    while bit < size:
        block = block + swapped(block, axis, size, bit)
        bit *= 2
    return block


def gather_blocks(block, axis, size):
    copies = jnp.broadcast_to(block[None], (size,) + block.shape)
    got = lax.all_to_all(copies, axis, split_axis=0, concat_axis=0, tiled=True)
    return got.reshape(size * block.shape[0], -1)


def with_tail(block, extra):
    return jnp.concatenate([block, jnp.full((8, block.shape[1]), extra)], axis=0)


def scatter_sum(whole, extra, axis, size):
    rows = whole.shape[0] // size
    parts = whole.reshape(size, rows, -1)
    tail = jnp.full((size, 8, whole.shape[1]), extra)
    parts = jnp.concatenate([parts, tail], axis=1)
    total = lax.all_to_all(parts, axis, split_axis=0, concat_axis=0, tiled=True).sum(axis=0)
    return total[:rows], total[rows, 0]


def per_device(n_rows, n_cols, kernels, pick_index, cell_index, counts, data):
    slots = kernels.shape[0]
    live = (lax.iota(jnp.int32, slots) < counts[0, 0]).astype(jnp.float32)
    pick_table = (pick_index[None, :] == lax.iota(jnp.int32, PBLK)[:, None]).astype(
        jnp.float32
    ) * live[None, :]
    cell_table = (cell_index[None, :] == lax.iota(jnp.int32, CBLK)[:, None]).astype(
        jnp.float32
    ) * live[None, :]

    def adjoint(group):
        product = jnp.einsum("kij,ki->kj", kernels, group[pick_index], precision=HIGHEST)
        whole = jnp.dot(cell_table, product, precision=HIGHEST)
        return scatter_sum(whole, jnp.sum(group * group), "rows", n_rows)

    def forward(owned):
        group = gather_blocks(owned, "rows", n_rows)
        product = jnp.einsum("kij,kj->ki", kernels, group[cell_index], precision=HIGHEST)
        whole = jnp.dot(pick_table, product, precision=HIGHEST)
        total = pairwise_sum(with_tail(whole, jnp.sum(group * group)), "cols", n_cols)
        return total[:PBLK], total[PBLK, 0]

    upick = gather_blocks(data, "cols", n_cols)
    product, square = adjoint(upick)
    beta = jnp.sqrt(square)
    vcell = product / beta
    phibar = beta
    rhobar = None
    model = jnp.zeros_like(vcell)
    search = None
    for step in range(ITERS):
        product, square = forward(vcell)
        alpha = jnp.sqrt(square)
        if step == 0:
            rhobar = alpha
            search = vcell / alpha
        else:
            theta = sine * alpha
            rhobar = -cosine * alpha
            search = vcell / alpha - theta / rho * search
        upick = product / alpha - alpha * (upick / beta)
        product, square = adjoint(upick)
        beta = jnp.sqrt(square)
        vcell = product / beta - beta * (vcell / alpha)
        rho = jnp.sqrt(rhobar * rhobar + beta * beta)
        cosine = rhobar / rho
        sine = beta / rho
        phi = cosine * phibar
        phibar = sine * phibar
        model = model + phi / rho * search
    square = jnp.full((8, 128), jnp.sum(vcell * vcell))
    square = pairwise_sum(square, "rows", n_rows)
    square = pairwise_sum(square, "cols", n_cols)
    alpha = jnp.sqrt(square[0, 0])
    search = vcell / alpha - sine * alpha / rho * search
    return (model, search)


def solution(mesh):
    def run(*args):
        return per_device(mesh.shape["rows"], mesh.shape["cols"], *args)

    return jax.shard_map(
        run,
        mesh=mesh,
        in_specs=(
            P(("rows", "cols"), None, None),
            P(("rows", "cols")),
            P(("rows", "cols")),
            P("rows", "cols"),
            P("cols", "rows"),
        ),
        out_specs=(P("rows", "cols"), P("rows", "cols")),
        check_vma=False,
    )
```

```python
import functools

import jax
import jax.numpy as jnp
from jax import lax
from jax.experimental import pallas as pl
from jax.experimental.pallas import tpu as pltpu
from jax.sharding import PartitionSpec as P

PBLK = 128
CBLK = 512
ITERS = 2
B = 128
SUB = 8
GROUP = 8
FOLDS = (1, 2, 4, 8)
TAIL = 8


def tile_transposed(tile, turned, pick):
    column = jnp.take_along_axis(turned, jnp.full((B, B), pick, jnp.int32), axis=1)
    return (tile * column).reshape(B // SUB, SUB, B).sum(axis=0)


def tile_forward(tile, row, masks):
    parts = [tile[SUB * q : SUB * (q + 1)] * row for q in range(B // SUB)]
    for bit, mask in zip(FOLDS, masks):
        parts = [
            jnp.where(mask, a, b) + pltpu.roll(jnp.where(mask, b, a), B - bit, 1)
            for a, b in zip(parts[::2], parts[1::2])
        ]
    return parts[0]


def over_tiles(slots, live, partial, target, spare, acc_ref):
    def some(group, carry):
        base = group * GROUP
        parts = [partial(base + k) for k in range(GROUP)]
        for k in range(GROUP):
            block = jnp.where(base + k < live, target(base + k), spare)
            where = pl.ds(pl.multiple_of(block * SUB, SUB), SUB)
            acc_ref[where, :] += parts[k]
        return carry

    acc_ref[...] = jnp.zeros_like(acc_ref)
    lax.fori_loop(0, (live + GROUP - 1) // GROUP, some, 0)


def strided_sum(ref, blocks):
    return sum(ref[pl.ds(k, blocks, stride=SUB), :] for k in range(SUB))


def halves(n_rows, cells):
    size = cells // n_rows
    return size, [range(core, n_rows, 2) for core in range(2)]


def adjoint_tail(n_rows, tiles, pick, cell, counts, u, keep, send, acc):
    turned = u.T
    over_tiles(
        tiles.shape[0],
        counts[0, 0],
        lambda s: tile_transposed(tiles[s], turned, pick[s]),
        lambda s: cell[s],
        CBLK,
        acc,
    )
    whole = strided_sum(acc, CBLK)
    square = jnp.full((TAIL, B), jnp.sum(u * u))
    size, _ = halves(n_rows, CBLK)
    core = lax.rem(lax.axis_index("rows"), 2)
    for block in range(n_rows):
        part = whole[block * size : (block + 1) * size]
        place = pl.ds(block // 2 * size, size)

        @pl.when(core == block % 2)
        def _():
            keep[place, :] = part

        @pl.when(core != block % 2)
        def _():
            send[place, :] = part

    keep[pl.ds(CBLK // 2, TAIL), :] = square
    send[pl.ds(CBLK // 2, TAIL), :] = square


def first_adjoint(n_rows, n_cols, tiles, pick, cell, counts, *rest):
    pieces, (u_out, keep, send, acc) = rest[:-4], rest[-4:]
    me = lax.axis_index("cols")
    offset = 0
    for piece in pieces:
        rows = PBLK // n_cols
        for at in range(piece.shape[0] // rows):
            owner = jnp.bitwise_xor(me, offset)
            u_out[pl.ds(pl.multiple_of(owner * rows, rows), rows), :] = piece[pl.ds(at * rows, rows), :]
            offset += 1
    adjoint_tail(n_rows, tiles, pick, cell, counts, u_out[...], keep, send, acc)


def next_adjoint(n_rows, tiles, pick, cell, counts, mine, other, u_old, beta_old, u_out, alpha_out, keep, send, acc):
    total = mine[...] + other[...]
    alpha = jnp.sqrt(total[PBLK:])
    alpha_out[...] = alpha
    u = total[:PBLK] / alpha[:1] - alpha[:1] * (u_old[...] / beta_old[:1])
    u_out[...] = u
    adjoint_tail(n_rows, tiles, pick, cell, counts, u, keep, send, acc)


def forward(first, n_rows, tiles, pick, cell, counts, mine, other, *rest):
    if first:
        v_out, beta_out, own_out, out, acc = rest
    else:
        v_old, alpha_old, v_out, beta_out, own_out, out, acc = rest
    size, _ = halves(n_rows, CBLK)
    me = lax.axis_index("rows")
    core = lax.rem(me, 2)
    beta = jnp.sqrt(mine[pl.ds(CBLK // 2, TAIL), :])
    beta_out[...] = beta
    for block in range(n_rows):
        place = pl.ds(block // 2 * size, size)
        part = jnp.where(core == block % 2, mine[place, :], other[place, :]) / beta[:1]
        here = pl.ds(block * size, size)
        if not first:
            part = part - beta[:1] * (v_old[here, :] / alpha_old[:1])
        v_out[here, :] = part
    own_out[...] = v_out[pl.ds(pl.multiple_of(me * size, size), size), :]
    lane = lax.broadcasted_iota(jnp.int32, (SUB, B), 1)
    masks = [jnp.bitwise_and(lane, bit) == 0 for bit in FOLDS]
    over_tiles(
        tiles.shape[0],
        counts[0, 0],
        lambda s: tile_forward(
            tiles[s], jnp.broadcast_to(v_out[pl.ds(cell[s], 1), :], (SUB, B)), masks
        ),
        lambda s: pick[s],
        PBLK,
        acc,
    )
    source = lax.broadcasted_iota(jnp.int32, (B, B), 0)
    column = lax.broadcasted_iota(jnp.int32, (B, B), 1)
    collect = (lax.rem(source, B // SUB) == lax.div(column, SUB)).astype(jnp.float32)
    sums = jnp.dot(
        acc[: PBLK * SUB, :],
        collect,
        precision=lax.Precision.HIGHEST,
        preferred_element_type=jnp.float32,
    )
    row = lax.rem(lax.broadcasted_iota(jnp.int32, (PBLK * SUB, B), 0), SUB)
    column = lax.rem(lax.broadcasted_iota(jnp.int32, (PBLK * SUB, B), 1), SUB)
    acc[: PBLK * SUB, :] = jnp.where(row == column, sums, 0.0)
    out[:PBLK, :] = strided_sum(acc, PBLK)
    v = v_out[...]
    out[pl.ds(PBLK, TAIL), :] = jnp.full((TAIL, B), jnp.sum(v * v))


def swapped(block, axis, size, bit):
    return lax.ppermute(block, axis, [(i, i ^ bit) for i in range(size)])


def pairwise_sum(block, axis, size, bit=1):
    while bit < size:
        block = block + swapped(block, axis, size, bit)
        bit *= 2
    return block


def shape(*dims):
    return jax.ShapeDtypeStruct(dims, jnp.float32)


def call(kernel, outs, blocks, scalars, arrays):
    vector = pl.BlockSpec(memory_space=pltpu.VMEM)
    scalar = pl.BlockSpec(memory_space=pltpu.SMEM)
    return pl.pallas_call(
        kernel,
        out_shape=outs,
        in_specs=[vector] + [scalar] * len(scalars) + [vector] * (len(arrays) - 1),
        out_specs=[vector] * len(outs),
        scratch_shapes=[pltpu.VMEM(((blocks + 1) * SUB, B), jnp.float32)],
        compiler_params=pltpu.CompilerParams(vmem_limit_bytes=24 << 20),
    )(arrays[0], *scalars, *arrays[1:])


def per_device(n_rows, n_cols, kernels, pick_index, cell_index, counts, data):
    tiles = pltpu.with_memory_space_constraint(kernels, pltpu.VMEM)
    scalars = (pick_index, cell_index, counts)
    half = CBLK // 2 + TAIL
    own = CBLK // n_rows

    def sum_cells(keep, send):
        return pairwise_sum(keep + swapped(send, "rows", n_rows, 1), "rows", n_rows, 2)

    pair = jnp.concatenate([data, swapped(data, "cols", n_cols, 1)], axis=0)
    pieces = [pair] + [swapped(pair, "cols", n_cols, bit) for bit in range(2, n_cols, 2)]
    upick, keep, send = call(
        functools.partial(first_adjoint, n_rows, n_cols),
        [shape(PBLK, B), shape(half, B), shape(half, B)],
        CBLK,
        scalars,
        [tiles] + pieces,
    )
    vcell = alpha = None
    blocks, alphas, betas = [], [], []
    for step in range(ITERS):
        mine = sum_cells(keep, send)
        other = swapped(mine, "rows", n_rows, 1)
        vcell, beta, block, product = call(
            functools.partial(forward, step == 0, n_rows),
            [shape(CBLK, B), shape(TAIL, B), shape(own, B), shape(PBLK + TAIL, B)],
            PBLK,
            scalars,
            [tiles, mine, other] + ([] if step == 0 else [vcell, alpha]),
        )
        blocks.append(block)
        betas.append(beta[0, 0])
        bit = 1
        while 2 * bit < n_cols:
            product = product + swapped(product, "cols", n_cols, bit)
            bit *= 2
        upick, alpha, keep, send = call(
            functools.partial(next_adjoint, n_rows),
            [shape(PBLK, B), shape(TAIL, B), shape(half, B), shape(half, B)],
            CBLK,
            scalars,
            [tiles, product, swapped(product, "cols", n_cols, bit), upick, beta],
        )
        alphas.append(alpha[0, 0])
    mine = sum_cells(keep, send)
    beta = jnp.sqrt(mine[CBLK // 2, 0])
    betas.append(beta)
    me = lax.axis_index("rows")
    old = vcell.reshape(n_rows // 2, 2, own, B)
    old = lax.dynamic_index_in_dim(old, lax.rem(me, 2), axis=1, keepdims=False)
    kept = mine[: CBLK // 2] / beta - beta * (old.reshape(CBLK // 2, B) / alphas[-1])
    square = jnp.full((TAIL, B), jnp.sum(kept * kept))
    square = square + swapped(square, "rows", n_rows, 1)
    square = pairwise_sum(square, "cols", n_cols)
    alphas.append(jnp.sqrt(square[0, 0]))
    blocks.append(lax.dynamic_slice_in_dim(kept, lax.div(me, 2) * own, own, axis=0))

    phibar, rhobar = betas[0], alphas[0]
    search = blocks[0] / alphas[0]
    model = jnp.zeros_like(search)
    for step in range(ITERS):
        beta, alpha = betas[step + 1], alphas[step + 1]
        rho = jnp.sqrt(rhobar * rhobar + beta * beta)
        cosine = rhobar / rho
        sine = beta / rho
        theta = sine * alpha
        rhobar = -cosine * alpha
        phi = cosine * phibar
        phibar = sine * phibar
        model = model + phi / rho * search
        search = blocks[step + 1] / alpha - theta / rho * search
    return (model, search)


def solution(mesh):
    def run(*args):
        return per_device(mesh.shape["rows"], mesh.shape["cols"], *args)

    return jax.shard_map(
        run,
        mesh=mesh,
        in_specs=(
            P(("rows", "cols"), None, None),
            P(("rows", "cols")),
            P(("rows", "cols")),
            P("rows", "cols"),
            P("cols", "rows"),
        ),
        out_specs=(P("rows", "cols"), P("rows", "cols")),
        check_vma=False,
    )
```

```python
import functools

import jax
import jax.numpy as jnp
from jax import lax
from jax.experimental import pallas as pl
from jax.experimental.pallas import tpu as pltpu
from jax.sharding import PartitionSpec as P

PBLK = 128
CBLK = 512
ITERS = 2
B = 128
SUB = 8
GROUP = 16
PARTS = 2
STEP = 16
BUFFERS = 4
TAIL = 8


def split(value):
    high = value.astype(jnp.bfloat16)
    return high, (value - high.astype(jnp.float32)).astype(jnp.bfloat16)


def split_tiles(start, tiles, out, held, arrived):
    steps = out.shape[0] // STEP

    def copy(step, slot):
        return pltpu.make_async_copy(
            tiles.at[pl.ds(start + step * STEP, STEP)], held.at[slot], arrived.at[slot]
        )

    for step in range(min(BUFFERS - 1, steps)):
        copy(step, step).start()
    for step in range(steps):
        slot = step % BUFFERS
        ahead = step + BUFFERS - 1
        if ahead < steps:
            copy(ahead, ahead % BUFFERS).start()
        copy(step, slot).wait()

        def one(k, carry):
            high, low = split(held[slot, k])
            out[step * STEP + k, :B, :] = high
            out[step * STEP + k, B:, :] = low
            return carry

        lax.fori_loop(0, STEP, one, 0, unroll=2)


def fill_table(table, value):
    high, low = split(value)
    blocks = value.shape[0]
    table[pl.ds(0, blocks, stride=SUB), :] = high.astype(jnp.float32)
    table[pl.ds(1, blocks, stride=SUB), :] = low.astype(jnp.float32)


def block_at(index):
    return pl.ds(pl.multiple_of(index * SUB, SUB), SUB)


def tile_transposed(tile, row):
    row = jnp.concatenate([row, row], axis=1)
    return jnp.dot(row, tile, preferred_element_type=jnp.float32)


def tile_forward(tile, row):
    both = lax.dot_general(
        row, tile, (((1,), (1,)), ((), ())), preferred_element_type=jnp.float32
    )
    return both[:, :B] + both[:, B:]


def over_tiles(parts, live, product, table, source, target, blocks, acc):
    zeros = jnp.zeros((blocks, B), jnp.float32)
    acc[pl.ds(0, blocks, stride=SUB), :] = zeros
    acc[pl.ds(1, blocks, stride=SUB), :] = zeros
    first = 0
    for tiles in parts:
        size = tiles.shape[0]
        here = jnp.clip(live - first, 0, size)

        def some(group, carry, tiles=tiles, first=first):
            base = group * GROUP
            sums = []
            for k in range(GROUP):
                row = table[block_at(source[first + base + k]), :].astype(jnp.bfloat16)
                sums.append(product(tiles[base + k], row))
            for k in range(GROUP):
                slot = first + base + k
                acc[block_at(jnp.where(slot < live, target[slot], blocks)), :] += sums[k]
            return carry

        lax.fori_loop(0, (here + GROUP - 1) // GROUP, some, 0)
        first += size
    return acc[pl.ds(0, blocks, stride=SUB), :] + acc[pl.ds(1, blocks, stride=SUB), :]


def halves(n_rows, cells):
    size = cells // n_rows
    return size, [range(core, n_rows, 2) for core in range(2)]


def adjoint_tail(n_rows, parts, pick, cell, counts, u, keep, send, table, acc):
    fill_table(table, u)
    whole = over_tiles(parts, counts[0, 0], tile_transposed, table, pick, cell, CBLK, acc)
    square = jnp.full((TAIL, B), jnp.sum(u * u))
    size, _ = halves(n_rows, CBLK)
    core = lax.rem(lax.axis_index("rows"), 2)
    for block in range(n_rows):
        part = whole[block * size : (block + 1) * size]
        place = pl.ds(block // 2 * size, size)

        @pl.when(core == block % 2)
        def _():
            keep[place, :] = part

        @pl.when(core != block % 2)
        def _():
            send[place, :] = part

    keep[pl.ds(CBLK // 2, TAIL), :] = square
    send[pl.ds(CBLK // 2, TAIL), :] = square


def first_adjoint(n_rows, n_cols, pick, cell, counts, *rest):
    parts, pieces, (u_out, keep, send, table, acc) = rest[:PARTS], rest[PARTS:-5], rest[-5:]
    me = lax.axis_index("cols")
    offset = 0
    for piece in pieces:
        rows = PBLK // n_cols
        for at in range(piece.shape[0] // rows):
            owner = jnp.bitwise_xor(me, offset)
            u_out[pl.ds(pl.multiple_of(owner * rows, rows), rows), :] = piece[pl.ds(at * rows, rows), :]
            offset += 1
    adjoint_tail(n_rows, parts, pick, cell, counts, u_out[...], keep, send, table, acc)


def next_adjoint(n_rows, pick, cell, counts, *rest):
    parts = rest[:PARTS]
    mine, other, u_old, beta_old, u_out, alpha_out, keep, send, table, acc = rest[PARTS:]
    total = mine[...] + other[...]
    alpha = jnp.sqrt(total[PBLK:])
    alpha_out[...] = alpha
    u = total[:PBLK] / alpha[:1] - alpha[:1] * (u_old[...] / beta_old[:1])
    u_out[...] = u
    adjoint_tail(n_rows, parts, pick, cell, counts, u, keep, send, table, acc)


def forward(first, n_rows, pick, cell, counts, *rest):
    parts, rest = rest[:PARTS], rest[PARTS:]
    if first:
        mine, other, v_out, beta_out, own_out, out, table, acc = rest
    else:
        mine, other, v_old, alpha_old, v_out, beta_out, own_out, out, table, acc = rest
    size, _ = halves(n_rows, CBLK)
    me = lax.axis_index("rows")
    core = lax.rem(me, 2)
    beta = jnp.sqrt(mine[pl.ds(CBLK // 2, TAIL), :])
    beta_out[...] = beta
    for block in range(n_rows):
        place = pl.ds(block // 2 * size, size)
        part = jnp.where(core == block % 2, mine[place, :], other[place, :]) / beta[:1]
        here = pl.ds(block * size, size)
        if not first:
            part = part - beta[:1] * (v_old[here, :] / alpha_old[:1])
        v_out[here, :] = part
    own_out[...] = v_out[pl.ds(pl.multiple_of(me * size, size), size), :]
    v = v_out[...]
    fill_table(table, v)
    out[:PBLK, :] = over_tiles(parts, counts[0, 0], tile_forward, table, cell, pick, PBLK, acc)
    out[pl.ds(PBLK, TAIL), :] = jnp.full((TAIL, B), jnp.sum(v * v))


def swapped(block, axis, size, bit):
    return lax.ppermute(block, axis, [(i, i ^ bit) for i in range(size)])


def pairwise_sum(block, axis, size, bit=1):
    while bit < size:
        block = block + swapped(block, axis, size, bit)
        bit *= 2
    return block


def shape(*dims):
    return jax.ShapeDtypeStruct(dims, jnp.float32)


VECTOR = pl.BlockSpec(memory_space=pltpu.VMEM)
SCALAR = pl.BlockSpec(memory_space=pltpu.SMEM)


def call(kernel, outs, sources, targets, scalars, arrays):
    return pl.pallas_call(
        kernel,
        out_shape=outs,
        in_specs=[SCALAR] * len(scalars) + [VECTOR] * len(arrays),
        out_specs=[VECTOR] * len(outs),
        scratch_shapes=[
            pltpu.VMEM((sources * SUB, B), jnp.float32),
            pltpu.VMEM(((targets + 1) * SUB, B), jnp.float32),
        ],
        compiler_params=pltpu.CompilerParams(vmem_limit_bytes=24 << 20),
    )(*scalars, *arrays)


def split_part(kernels, part):
    size = kernels.shape[0] // PARTS
    return pl.pallas_call(
        functools.partial(split_tiles, part * size),
        out_shape=pltpu.VMEM((size, 2 * B, B), jnp.bfloat16),
        in_specs=[pl.BlockSpec(memory_space=pl.ANY)],
        out_specs=VECTOR,
        scratch_shapes=[
            pltpu.VMEM((BUFFERS, STEP, B, B), jnp.float32),
            pltpu.SemaphoreType.DMA((BUFFERS,)),
        ],
        cost_estimate=pl.CostEstimate(
            flops=4 * size * B * B, bytes_accessed=4 * size * B * B, transcendentals=0
        ),
        compiler_params=pltpu.CompilerParams(vmem_limit_bytes=24 << 20),
    )(kernels)


def per_device(n_rows, n_cols, kernels, pick_index, cell_index, counts, data):
    tiles = [split_part(kernels, part) for part in range(PARTS)]
    scalars = tuple(
        pltpu.with_memory_space_constraint(x, pltpu.SMEM) for x in (pick_index, cell_index, counts)
    )
    half = CBLK // 2 + TAIL
    own = CBLK // n_rows

    def sum_cells(keep, send):
        return pairwise_sum(keep + swapped(send, "rows", n_rows, 1), "rows", n_rows, 2)

    pair = jnp.concatenate([data, swapped(data, "cols", n_cols, 1)], axis=0)
    pieces = [pair] + [swapped(pair, "cols", n_cols, bit) for bit in range(2, n_cols, 2)]
    upick, keep, send = call(
        functools.partial(first_adjoint, n_rows, n_cols),
        [shape(PBLK, B), shape(half, B), shape(half, B)],
        PBLK,
        CBLK,
        scalars,
        tiles + pieces,
    )
    vcell = alpha = None
    blocks, alphas, betas = [], [], []
    for step in range(ITERS):
        mine = sum_cells(keep, send)
        other = swapped(mine, "rows", n_rows, 1)
        vcell, beta, block, product = call(
            functools.partial(forward, step == 0, n_rows),
            [shape(CBLK, B), shape(TAIL, B), shape(own, B), shape(PBLK + TAIL, B)],
            CBLK,
            PBLK,
            scalars,
            tiles + [mine, other] + ([] if step == 0 else [vcell, alpha]),
        )
        blocks.append(block)
        betas.append(beta[0, 0])
        bit = 1
        while 2 * bit < n_cols:
            product = product + swapped(product, "cols", n_cols, bit)
            bit *= 2
        upick, alpha, keep, send = call(
            functools.partial(next_adjoint, n_rows),
            [shape(PBLK, B), shape(TAIL, B), shape(half, B), shape(half, B)],
            PBLK,
            CBLK,
            scalars,
            tiles + [product, swapped(product, "cols", n_cols, bit), upick, beta],
        )
        alphas.append(alpha[0, 0])
    mine = sum_cells(keep, send)
    beta = jnp.sqrt(mine[CBLK // 2, 0])
    betas.append(beta)
    me = lax.axis_index("rows")
    old = vcell.reshape(n_rows // 2, 2, own, B)
    old = lax.dynamic_index_in_dim(old, lax.rem(me, 2), axis=1, keepdims=False)
    kept = mine[: CBLK // 2] / beta - beta * (old.reshape(CBLK // 2, B) / alphas[-1])
    square = jnp.full((TAIL, B), jnp.sum(kept * kept))
    square = square + swapped(square, "rows", n_rows, 1)
    square = pairwise_sum(square, "cols", n_cols)
    alphas.append(jnp.sqrt(square[0, 0]))
    blocks.append(lax.dynamic_slice_in_dim(kept, lax.div(me, 2) * own, own, axis=0))

    phibar, rhobar = betas[0], alphas[0]
    search = blocks[0] / alphas[0]
    model = jnp.zeros_like(search)
    for step in range(ITERS):
        beta, alpha = betas[step + 1], alphas[step + 1]
        rho = jnp.sqrt(rhobar * rhobar + beta * beta)
        cosine = rhobar / rho
        sine = beta / rho
        theta = sine * alpha
        rhobar = -cosine * alpha
        phi = cosine * phibar
        phibar = sine * phibar
        model = model + phi / rho * search
        search = blocks[step + 1] / alpha - theta / rho * search
    return (model, search)


def solution(mesh):
    def run(*args):
        return per_device(mesh.shape["rows"], mesh.shape["cols"], *args)

    return jax.shard_map(
        run,
        mesh=mesh,
        in_specs=(
            P(("rows", "cols"), None, None),
            P(("rows", "cols")),
            P(("rows", "cols")),
            P("rows", "cols"),
            P("cols", "rows"),
        ),
        out_specs=(P("rows", "cols"), P("rows", "cols")),
        check_vma=False,
    )
```

```python
import functools

import jax
import jax.numpy as jnp
from jax import lax
from jax.experimental import pallas as pl
from jax.experimental.pallas import tpu as pltpu
from jax.sharding import PartitionSpec as P

PBLK = 128
CBLK = 512
ITERS = 2
B = 128
SUB = 8
GROUP = 16
PARTS = 2
STEP = 16
BUFFERS = 4
TAIL = 8


def split(value):
    high = value.astype(jnp.bfloat16)
    return high, (value - high.astype(jnp.float32)).astype(jnp.bfloat16)


def split_tiles(start, tiles, data, out, data_out, held, arrived):
    steps = out.shape[0] // STEP
    data_out[...] = data[...]

    def copy(step, slot):
        return pltpu.make_async_copy(
            tiles.at[pl.ds(start + step * STEP, STEP)], held.at[slot], arrived.at[slot]
        )

    for step in range(min(BUFFERS - 1, steps)):
        copy(step, step).start()
    for step in range(steps):
        slot = step % BUFFERS
        ahead = step + BUFFERS - 1
        if ahead < steps:
            copy(ahead, ahead % BUFFERS).start()
        copy(step, slot).wait()

        def one(k, carry):
            high, low = split(held[slot, k])
            out[step * STEP + k, :B, :] = high
            out[step * STEP + k, B:, :] = low
            return carry

        lax.fori_loop(0, STEP, one, 0, unroll=4)


def rows_of(ref, start, blocks):
    return ref.at[pl.ds(start, blocks, stride=SUB), :]


def fill_table(table, value):
    high, low = split(value)
    blocks = value.shape[0]
    for start, term in enumerate((high, low, high, low)):
        rows_of(table, start, blocks)[...] = term.astype(jnp.float32)


def block_at(index):
    return pl.ds(pl.multiple_of(index * SUB, SUB), SUB)


def pair_transposed(tiles, one, two, first):
    row = jnp.where(first, one, two).astype(jnp.bfloat16)
    row = jnp.concatenate([row, row], axis=1)
    both = jnp.dot(row, tiles, preferred_element_type=jnp.float32)
    return both[:, :B], both[:, B:]


def pair_forward(tiles, one, two, first):
    zero = jnp.zeros_like(one)
    row = jnp.concatenate([jnp.where(first, one, zero), jnp.where(first, zero, two)], axis=1)
    both = lax.dot_general(
        row.astype(jnp.bfloat16),
        tiles,
        (((1,), (1,)), ((), ())),
        preferred_element_type=jnp.float32,
    )
    both = both[:, :B] + both[:, B:]
    return both, both


def over_tiles(parts, live, product, table, source, target, blocks, accs):
    places = [(accs[0], 0), (accs[0], 1), (accs[1], 2), (accs[1], 3)]
    for acc, start in places:
        rows_of(acc, start, blocks)[...] = jnp.zeros((blocks, B), jnp.float32)
    upper = lax.broadcasted_iota(jnp.int32, (SUB, B), 0) < 2
    first = 0
    for tiles in parts:
        size = tiles.shape[0]
        here = jnp.clip(live - first, 0, size)

        def some(group, carry, tiles=tiles, first=first):
            base = group * GROUP
            sums = []
            for k in range(0, GROUP, 2):
                slot = first + base + k
                pair = jnp.concatenate([tiles[base + k], tiles[base + k + 1]], axis=1)
                one, two = (table[block_at(source[slot + n]), :] for n in range(2))
                sums.append(product(pair, one, two, upper))
            for k in range(GROUP):
                slot = first + base + k
                place = block_at(jnp.where(slot < live, target[slot], blocks))
                accs[k % 2][place, :] += sums[k // 2][k % 2]
            return carry

        lax.fori_loop(0, (here + GROUP - 1) // GROUP, some, 0)
        first += size
    return sum(rows_of(acc, start, blocks)[...] for acc, start in places)


def halves(n_rows, cells):
    size = cells // n_rows
    return size, [range(core, n_rows, 2) for core in range(2)]


def adjoint_tail(n_rows, parts, pick, cell, counts, u, keep, send, table, *accs):
    fill_table(table, u)
    whole = over_tiles(parts, counts[0, 0], pair_transposed, table, pick, cell, CBLK, accs)
    square = jnp.full((TAIL, B), jnp.sum(u * u))
    size, _ = halves(n_rows, CBLK)
    core = lax.rem(lax.axis_index("rows"), 2)
    for block in range(n_rows):
        part = whole[block * size : (block + 1) * size]
        place = pl.ds(block // 2 * size, size)

        @pl.when(core == block % 2)
        def _():
            keep[place, :] = part

        @pl.when(core != block % 2)
        def _():
            send[place, :] = part

    keep[pl.ds(CBLK // 2, TAIL), :] = square
    send[pl.ds(CBLK // 2, TAIL), :] = square


def first_adjoint(n_rows, n_cols, pick, cell, counts, *rest):
    parts, pieces, (u_out, keep, send, table, *accs) = rest[:PARTS], rest[PARTS:-6], rest[-6:]
    me = lax.axis_index("cols")
    offset = 0
    for piece in pieces:
        rows = PBLK // n_cols
        for at in range(piece.shape[0] // rows):
            owner = jnp.bitwise_xor(me, offset)
            u_out[pl.ds(pl.multiple_of(owner * rows, rows), rows), :] = piece[pl.ds(at * rows, rows), :]
            offset += 1
    adjoint_tail(n_rows, parts, pick, cell, counts, u_out[...], keep, send, table, *accs)


def next_adjoint(n_rows, pick, cell, counts, *rest):
    parts = rest[:PARTS]
    mine, other, u_old, beta_old, u_out, alpha_out, keep, send, table, *accs = rest[PARTS:]
    total = mine[...] + other[...]
    alpha = jnp.sqrt(total[PBLK:])
    alpha_out[...] = alpha
    u = total[:PBLK] / alpha[:1] - alpha[:1] * (u_old[...] / beta_old[:1])
    u_out[...] = u
    adjoint_tail(n_rows, parts, pick, cell, counts, u, keep, send, table, *accs)


def cell_vector(n_rows, mine, other, v_old, alpha_old, v_out, beta_out, own_out):
    size, _ = halves(n_rows, CBLK)
    me = lax.axis_index("rows")
    core = lax.rem(me, 2)
    beta = jnp.sqrt(mine[pl.ds(CBLK // 2, TAIL), :])
    beta_out[...] = beta
    for block in range(n_rows):
        place = pl.ds(block // 2 * size, size)
        part = jnp.where(core == block % 2, mine[place, :], other[place, :]) / beta[:1]
        here = pl.ds(block * size, size)
        if v_old is not None:
            part = part - beta[:1] * (v_old[here, :] / alpha_old[:1])
        v_out[here, :] = part
    own_out[...] = v_out[pl.ds(pl.multiple_of(me * size, size), size), :]
    v = v_out[...]
    return v, jnp.full((TAIL, B), jnp.sum(v * v))


def forward(first, n_rows, pick, cell, counts, *rest):
    parts, rest = rest[:PARTS], rest[PARTS:]
    old = (None, None) if first else rest[2:4]
    v_out, beta_out, own_out, out, table, *accs = rest[-7:]
    v, square = cell_vector(n_rows, rest[0], rest[1], *old, v_out, beta_out, own_out)
    fill_table(table, v)
    out[:PBLK, :] = over_tiles(parts, counts[0, 0], pair_forward, table, cell, pick, PBLK, accs)
    out[pl.ds(PBLK, TAIL), :] = square


def last_vector(n_rows, mine, other, v_old, alpha_old, v_out, beta_out, own_out, square_out):
    _, square_out[...] = cell_vector(
        n_rows, mine, other, v_old, alpha_old, v_out, beta_out, own_out
    )


def finish(*refs):
    blocks, refs = refs[: ITERS + 1], refs[ITERS + 1 :]
    betas, refs = refs[: ITERS + 1], refs[ITERS + 1 :]
    alphas, refs = refs[:ITERS], refs[ITERS:]
    squares, (model_out, search_out) = refs[:-2], refs[-2:]
    betas = [ref[:1] for ref in betas]
    alphas = [ref[:1] for ref in alphas] + [jnp.sqrt(sum(ref[:1] for ref in squares))]
    phibar, rhobar = betas[0], alphas[0]
    search = blocks[0][...] / alphas[0]
    model = jnp.zeros_like(search)
    for step in range(ITERS):
        beta, alpha = betas[step + 1], alphas[step + 1]
        rho = jnp.sqrt(rhobar * rhobar + beta * beta)
        cosine = rhobar / rho
        sine = beta / rho
        theta = sine * alpha
        rhobar = -cosine * alpha
        phi = cosine * phibar
        phibar = sine * phibar
        model = model + phi / rho * search
        search = blocks[step + 1][...] / alpha - theta / rho * search
    model_out[...] = model
    search_out[...] = search


def swapped(block, axis, size, bit):
    return lax.ppermute(block, axis, [(i, i ^ bit) for i in range(size)])


def shape(*dims):
    return jax.ShapeDtypeStruct(dims, jnp.float32)


VECTOR = pl.BlockSpec(memory_space=pltpu.VMEM)
SCALAR = pl.BlockSpec(memory_space=pltpu.SMEM)


def call(kernel, outs, sources, targets, scalars, arrays):
    return pl.pallas_call(
        kernel,
        out_shape=outs,
        in_specs=[SCALAR] * len(scalars) + [VECTOR] * len(arrays),
        out_specs=[VECTOR] * len(outs),
        scratch_shapes=[
            pltpu.VMEM((sources * SUB, B), jnp.float32),
            pltpu.VMEM(((targets + 1) * SUB, B), jnp.float32),
            pltpu.VMEM(((targets + 1) * SUB, B), jnp.float32),
        ],
        compiler_params=pltpu.CompilerParams(vmem_limit_bytes=24 << 20),
    )(*scalars, *arrays)


def split_part(kernels, data, part):
    size = kernels.shape[0] // PARTS
    return pl.pallas_call(
        functools.partial(split_tiles, part * size),
        out_shape=[pltpu.VMEM((size, 2 * B, B), jnp.bfloat16), shape(*data.shape)],
        in_specs=[pl.BlockSpec(memory_space=pl.ANY), VECTOR],
        out_specs=[VECTOR, VECTOR],
        scratch_shapes=[
            pltpu.VMEM((BUFFERS, STEP, B, B), jnp.float32),
            pltpu.SemaphoreType.DMA((BUFFERS,)),
        ],
        cost_estimate=pl.CostEstimate(
            flops=4 * size * B * B, bytes_accessed=4 * size * B * B, transcendentals=0
        ),
        compiler_params=pltpu.CompilerParams(vmem_limit_bytes=24 << 20),
    )(kernels, data)


def simple_call(kernel, outs, arrays):
    return pl.pallas_call(
        kernel,
        out_shape=outs,
        in_specs=[VECTOR] * len(arrays),
        out_specs=[VECTOR] * len(outs),
    )(*arrays)


def per_device(n_rows, n_cols, kernels, pick_index, cell_index, counts, data):
    scalars = (pick_index, cell_index, counts)
    half = CBLK // 2 + TAIL
    own = CBLK // n_rows

    def sum_cells(keep, send):
        mine = keep + swapped(send, "rows", n_rows, 1)
        bit = 2
        while bit < n_rows:
            mine = mine + swapped(mine, "rows", n_rows, bit)
            bit *= 2
        return [mine, swapped(mine, "rows", n_rows, 1)]

    partner = swapped(data, "cols", n_cols, 1)
    tiles = [None] * PARTS
    tiles[0], passed = split_part(kernels, data, 0)
    for part in range(1, PARTS):
        tiles[part], _ = split_part(kernels, data, part)
    pair = jnp.concatenate([passed, partner], axis=0)
    pieces = [pair] + [swapped(pair, "cols", n_cols, bit) for bit in range(2, n_cols, 2)]
    upick, keep, send = call(
        functools.partial(first_adjoint, n_rows, n_cols),
        [shape(PBLK, B), shape(half, B), shape(half, B)],
        PBLK,
        CBLK,
        scalars,
        tiles + pieces,
    )
    old = []
    blocks, alphas, betas = [], [], []
    for step in range(ITERS):
        vcell, beta, block, product = call(
            functools.partial(forward, step == 0, n_rows),
            [shape(CBLK, B), shape(TAIL, B), shape(own, B), shape(PBLK + TAIL, B)],
            CBLK,
            PBLK,
            scalars,
            tiles + sum_cells(keep, send) + old,
        )
        blocks.append(block)
        betas.append(beta)
        bit = 1
        while 2 * bit < n_cols:
            product = product + swapped(product, "cols", n_cols, bit)
            bit *= 2
        upick, alpha, keep, send = call(
            functools.partial(next_adjoint, n_rows),
            [shape(PBLK, B), shape(TAIL, B), shape(half, B), shape(half, B)],
            PBLK,
            CBLK,
            scalars,
            tiles + [product, swapped(product, "cols", n_cols, bit), upick, beta],
        )
        alphas.append(alpha)
        old = [vcell, alpha]
    _, beta, block, square = simple_call(
        functools.partial(last_vector, n_rows),
        [shape(CBLK, B), shape(TAIL, B), shape(own, B), shape(TAIL, B)],
        sum_cells(keep, send) + old,
    )
    blocks.append(block)
    betas.append(beta)
    square = square + swapped(square, "cols", n_cols, 1)
    squares = [square] + [swapped(square, "cols", n_cols, bit) for bit in range(2, n_cols, 2)]
    model, search = simple_call(
        finish, [shape(own, B), shape(own, B)], blocks + betas + alphas + squares
    )
    return (model, search)


def solution(mesh):
    def run(*args):
        return per_device(mesh.shape["rows"], mesh.shape["cols"], *args)

    return jax.shard_map(
        run,
        mesh=mesh,
        in_specs=(
            P(("rows", "cols"), None, None),
            P(("rows", "cols")),
            P(("rows", "cols")),
            P("rows", "cols"),
            P("cols", "rows"),
        ),
        out_specs=(P("rows", "cols"), P("rows", "cols")),
        check_vma=False,
    )
```

```python
import functools

import jax
import jax.numpy as jnp
from jax import lax
from jax.experimental import pallas as pl
from jax.experimental.pallas import tpu as pltpu
from jax.sharding import PartitionSpec as P

PBLK = 128
CBLK = 512
ITERS = 2
B = 128
SUB = 8
GROUP = 16
PARTS = 2
STEP = 8
BUFFERS = 6
UNITS = 2
TAIL = 8
EXTRA = 3


def split(value):
    high = value.astype(jnp.bfloat16)
    return high, (value - high.astype(jnp.float32)).astype(jnp.bfloat16)


def split_tiles(start, tiles, data, out, data_out, held, arrived):
    steps = out.shape[0] // STEP
    data_out[...] = data[...]

    def copy(step, slot):
        return pltpu.make_async_copy(
            tiles.at[pl.ds(start + step * STEP, STEP)], held.at[slot], arrived.at[slot]
        )

    for step in range(min(BUFFERS - 1, steps)):
        copy(step, step).start()
    for step in range(steps):
        slot = step % BUFFERS
        ahead = step + BUFFERS - 1
        if ahead < steps:
            copy(ahead, ahead % BUFFERS).start()
        copy(step, slot).wait()

        def one(k, carry):
            high, low = split(held[slot, k])
            out[step * STEP + k, :B, :] = high
            out[step * STEP + k, B:, :] = low
            return carry

        lax.fori_loop(0, STEP, one, 0, unroll=4)


def rows_of(ref, start, blocks):
    return ref.at[pl.ds(start, blocks, stride=SUB), :]


def fill_table(table, value):
    high, low = split(value)
    blocks = value.shape[0]
    for start, term in enumerate((high, low, high, low)):
        rows_of(table, start, blocks)[...] = term.astype(jnp.float32)


def block_at(index):
    return pl.ds(pl.multiple_of(index * SUB, SUB), SUB)


def twice(rows):
    return jnp.concatenate([rows, rows], axis=0).astype(jnp.bfloat16)


def pair_row_transposed(one, two, first):
    row = twice(jnp.where(first, one, two))
    return jnp.concatenate([row, row], axis=1)


def pair_row_forward(one, two, first):
    zero = jnp.zeros_like(one)
    return jnp.concatenate(
        [twice(jnp.where(first, one, zero)), twice(jnp.where(first, zero, two))], axis=1
    )


def over_tiles(parts, live, forward, table, source, target, blocks, accs):
    places = [(accs[0], 0), (accs[0], 1), (accs[1], 2), (accs[1], 3)]
    for acc, start in places:
        rows_of(acc, start, blocks)[...] = jnp.zeros((blocks, B), jnp.float32)
    upper = lax.broadcasted_iota(jnp.int32, (SUB, B), 0) < 2
    first = 0
    for tiles in parts:
        size = tiles.shape[0]
        here = jnp.clip(live - first, 0, size)

        def some(group, carry, tiles=tiles, first=first):
            kinds = [pltpu.ACC(k % UNITS)((2 * SUB, 2 * B), jnp.float32) for k in range(GROUP // 2)]
            pl.run_scoped(functools.partial(multiply, group, tiles, first), *kinds)
            return carry

        def multiply(group, tiles, first, *units):
            base = group * GROUP
            sums = []
            for k in range(0, GROUP, 2):
                slot = first + base + k
                at, unit = divmod(k // 2, UNITS)
                pair = jnp.concatenate([tiles[base + k], tiles[base + k + 1]], axis=1)
                pltpu.matmul_push_rhs(pair, at % 2, unit, transpose=forward)
                one, two = (table[block_at(source[slot + n]), :] for n in range(2))
                row = (pair_row_forward if forward else pair_row_transposed)(one, two, upper)
                pltpu.matmul_acc_lhs(units[k // 2], row, load_staged_rhs=at % 2)
            for k in range(0, GROUP, 2):
                both = pltpu.matmul_pop(units[k // 2])[:SUB]
                if forward:
                    both = both[:, :B] + both[:, B:]
                    sums.append((both, both))
                else:
                    sums.append((both[:, :B], both[:, B:]))
            for k in range(GROUP):
                slot = first + base + k
                place = block_at(jnp.where(slot < live, target[slot], blocks))
                accs[k % 2][place, :] += sums[k // 2][k % 2]

        lax.fori_loop(0, (here + GROUP - 1) // GROUP, some, 0)
        first += size
    return sum(rows_of(acc, start, blocks)[...] for acc, start in places)


def halves(n_rows, cells):
    size = cells // n_rows
    return size, [range(core, n_rows, 2) for core in range(2)]


def adjoint_tail(n_rows, parts, pick, cell, counts, u, keep, send, table, *accs):
    fill_table(table, u)
    whole = over_tiles(parts, counts[0, 0], False, table, pick, cell, CBLK, accs)
    square = jnp.full((TAIL, B), jnp.sum(u * u))
    size, _ = halves(n_rows, CBLK)
    core = lax.rem(lax.axis_index("rows"), 2)
    for block in range(n_rows):
        part = whole[block * size : (block + 1) * size]
        place = pl.ds(block // 2 * size, size)

        @pl.when(core == block % 2)
        def _():
            keep[place, :] = part

        @pl.when(core != block % 2)
        def _():
            send[place, :] = part

    keep[pl.ds(CBLK // 2, TAIL), :] = square
    send[pl.ds(CBLK // 2, TAIL), :] = square


def first_adjoint(n_rows, n_cols, pick, cell, counts, *rest):
    parts, pieces, (u_out, keep, send, table, *accs) = rest[:PARTS], rest[PARTS:-EXTRA - 3], rest[-EXTRA - 3 :]
    me = lax.axis_index("cols")
    offset = 0
    for piece in pieces:
        rows = PBLK // n_cols
        for at in range(piece.shape[0] // rows):
            owner = jnp.bitwise_xor(me, offset)
            u_out[pl.ds(pl.multiple_of(owner * rows, rows), rows), :] = piece[pl.ds(at * rows, rows), :]
            offset += 1
    adjoint_tail(n_rows, parts, pick, cell, counts, u_out[...], keep, send, table, *accs)


def next_adjoint(n_rows, pick, cell, counts, *rest):
    parts = rest[:PARTS]
    mine, other, u_old, beta_old, u_out, alpha_out, keep, send, table, *accs = rest[PARTS:]
    total = mine[...] + other[...]
    alpha = jnp.sqrt(total[PBLK:])
    alpha_out[...] = alpha
    u = total[:PBLK] / alpha[:1] - alpha[:1] * (u_old[...] / beta_old[:1])
    u_out[...] = u
    adjoint_tail(n_rows, parts, pick, cell, counts, u, keep, send, table, *accs)


def cell_vector(n_rows, mine, other, v_old, alpha_old, v_out, beta_out, own_out):
    size, _ = halves(n_rows, CBLK)
    me = lax.axis_index("rows")
    core = lax.rem(me, 2)
    beta = jnp.sqrt(mine[pl.ds(CBLK // 2, TAIL), :])
    beta_out[...] = beta
    for block in range(n_rows):
        place = pl.ds(block // 2 * size, size)
        part = jnp.where(core == block % 2, mine[place, :], other[place, :]) / beta[:1]
        here = pl.ds(block * size, size)
        if v_old is not None:
            part = part - beta[:1] * (v_old[here, :] / alpha_old[:1])
        v_out[here, :] = part
    own_out[...] = v_out[pl.ds(pl.multiple_of(me * size, size), size), :]
    v = v_out[...]
    return v, jnp.full((TAIL, B), jnp.sum(v * v))


def forward(first, n_rows, pick, cell, counts, *rest):
    parts, rest = rest[:PARTS], rest[PARTS:]
    old = (None, None) if first else rest[2:4]
    v_out, beta_out, own_out, out, table, *accs = rest[-EXTRA - 4 :]
    v, square = cell_vector(n_rows, rest[0], rest[1], *old, v_out, beta_out, own_out)
    fill_table(table, v)
    out[:PBLK, :] = over_tiles(parts, counts[0, 0], True, table, cell, pick, PBLK, accs)
    out[pl.ds(PBLK, TAIL), :] = square


def last_vector(n_rows, mine, other, v_old, alpha_old, v_out, beta_out, own_out, square_out):
    _, square_out[...] = cell_vector(
        n_rows, mine, other, v_old, alpha_old, v_out, beta_out, own_out
    )


def finish(*refs):
    blocks, refs = refs[: ITERS + 1], refs[ITERS + 1 :]
    betas, refs = refs[: ITERS + 1], refs[ITERS + 1 :]
    alphas, refs = refs[:ITERS], refs[ITERS:]
    squares, (model_out, search_out) = refs[:-2], refs[-2:]
    betas = [ref[:1] for ref in betas]
    alphas = [ref[:1] for ref in alphas] + [jnp.sqrt(sum(ref[:1] for ref in squares))]
    phibar, rhobar = betas[0], alphas[0]
    search = blocks[0][...] / alphas[0]
    model = jnp.zeros_like(search)
    for step in range(ITERS):
        beta, alpha = betas[step + 1], alphas[step + 1]
        rho = jnp.sqrt(rhobar * rhobar + beta * beta)
        cosine = rhobar / rho
        sine = beta / rho
        theta = sine * alpha
        rhobar = -cosine * alpha
        phi = cosine * phibar
        phibar = sine * phibar
        model = model + phi / rho * search
        search = blocks[step + 1][...] / alpha - theta / rho * search
    model_out[...] = model
    search_out[...] = search


def swapped(block, axis, size, bit):
    return lax.ppermute(block, axis, [(i, i ^ bit) for i in range(size)])


def shape(*dims):
    return jax.ShapeDtypeStruct(dims, jnp.float32)


VECTOR = pl.BlockSpec(memory_space=pltpu.VMEM)
SCALAR = pl.BlockSpec(memory_space=pltpu.SMEM)


def call(kernel, outs, sources, targets, scalars, arrays):
    return pl.pallas_call(
        kernel,
        out_shape=outs,
        in_specs=[SCALAR] * len(scalars) + [VECTOR] * len(arrays),
        out_specs=[VECTOR] * len(outs),
        scratch_shapes=[
            pltpu.VMEM((sources * SUB, B), jnp.float32),
            pltpu.VMEM(((targets + 1) * SUB, B), jnp.float32),
            pltpu.VMEM(((targets + 1) * SUB, B), jnp.float32),
        ],
        compiler_params=pltpu.CompilerParams(vmem_limit_bytes=24 << 20),
    )(*scalars, *arrays)


def split_part(kernels, data, part):
    size = kernels.shape[0] // PARTS
    return pl.pallas_call(
        functools.partial(split_tiles, part * size),
        out_shape=[pltpu.VMEM((size, 2 * B, B), jnp.bfloat16), shape(*data.shape)],
        in_specs=[pl.BlockSpec(memory_space=pl.ANY), VECTOR],
        out_specs=[VECTOR, VECTOR],
        scratch_shapes=[
            pltpu.VMEM((BUFFERS, STEP, B, B), jnp.float32),
            pltpu.SemaphoreType.DMA((BUFFERS,)),
        ],
        cost_estimate=pl.CostEstimate(
            flops=4 * size * B * B, bytes_accessed=4 * size * B * B, transcendentals=0
        ),
        compiler_params=pltpu.CompilerParams(vmem_limit_bytes=24 << 20),
    )(kernels, data)


def simple_call(kernel, outs, arrays):
    return pl.pallas_call(
        kernel,
        out_shape=outs,
        in_specs=[VECTOR] * len(arrays),
        out_specs=[VECTOR] * len(outs),
    )(*arrays)


def per_device(n_rows, n_cols, kernels, pick_index, cell_index, counts, data):
    scalars = (pick_index, cell_index, counts)
    half = CBLK // 2 + TAIL
    own = CBLK // n_rows

    def sum_cells(keep, send):
        mine = keep + swapped(send, "rows", n_rows, 1)
        bit = 2
        while bit < n_rows:
            mine = mine + swapped(mine, "rows", n_rows, bit)
            bit *= 2
        return [mine, swapped(mine, "rows", n_rows, 1)]

    partner = swapped(data, "cols", n_cols, 1)
    tiles = [None] * PARTS
    tiles[0], passed = split_part(kernels, data, 0)
    for part in range(1, PARTS):
        tiles[part], _ = split_part(kernels, data, part)
    pair = jnp.concatenate([passed, partner], axis=0)
    pieces = [pair] + [swapped(pair, "cols", n_cols, bit) for bit in range(2, n_cols, 2)]
    upick, keep, send = call(
        functools.partial(first_adjoint, n_rows, n_cols),
        [shape(PBLK, B), shape(half, B), shape(half, B)],
        PBLK,
        CBLK,
        scalars,
        tiles + pieces,
    )
    old = []
    blocks, alphas, betas = [], [], []
    for step in range(ITERS):
        vcell, beta, block, product = call(
            functools.partial(forward, step == 0, n_rows),
            [shape(CBLK, B), shape(TAIL, B), shape(own, B), shape(PBLK + TAIL, B)],
            CBLK,
            PBLK,
            scalars,
            tiles + sum_cells(keep, send) + old,
        )
        blocks.append(block)
        betas.append(beta)
        bit = 1
        while 2 * bit < n_cols:
            product = product + swapped(product, "cols", n_cols, bit)
            bit *= 2
        upick, alpha, keep, send = call(
            functools.partial(next_adjoint, n_rows),
            [shape(PBLK, B), shape(TAIL, B), shape(half, B), shape(half, B)],
            PBLK,
            CBLK,
            scalars,
            tiles + [product, swapped(product, "cols", n_cols, bit), upick, beta],
        )
        alphas.append(alpha)
        old = [vcell, alpha]
    _, beta, block, square = simple_call(
        functools.partial(last_vector, n_rows),
        [shape(CBLK, B), shape(TAIL, B), shape(own, B), shape(TAIL, B)],
        sum_cells(keep, send) + old,
    )
    blocks.append(block)
    betas.append(beta)
    square = square + swapped(square, "cols", n_cols, 1)
    squares = [square] + [swapped(square, "cols", n_cols, bit) for bit in range(2, n_cols, 2)]
    model, search = simple_call(
        finish, [shape(own, B), shape(own, B)], blocks + betas + alphas + squares
    )
    return (model, search)


def solution(mesh):
    def run(*args):
        return per_device(mesh.shape["rows"], mesh.shape["cols"], *args)

    return jax.shard_map(
        run,
        mesh=mesh,
        in_specs=(
            P(("rows", "cols"), None, None),
            P(("rows", "cols")),
            P(("rows", "cols")),
            P("rows", "cols"),
            P("cols", "rows"),
        ),
        out_specs=(P("rows", "cols"), P("rows", "cols")),
        check_vma=False,
    )
```

```python
import functools

import jax
import jax.numpy as jnp
from jax import lax
from jax.experimental import pallas as pl
from jax.experimental.pallas import tpu as pltpu
from jax.sharding import PartitionSpec as P

PBLK = 128
CBLK = 512
ITERS = 2
B = 128
SUB = 8
GROUP = 32
PARTS = 2
STEP = 32
BUFFERS = 3
TAIL = 8


def split(value):
    high = value.astype(jnp.bfloat16)
    return high, (value - high.astype(jnp.float32)).astype(jnp.bfloat16)


def split_tiles(start, tiles, data, out, data_out, held, arrived):
    steps = out.shape[0] // STEP
    data_out[...] = data[...]

    def copy(step, slot):
        return pltpu.make_async_copy(
            tiles.at[pl.ds(start + step * STEP, STEP)], held.at[slot], arrived.at[slot]
        )

    for step in range(min(BUFFERS - 1, steps)):
        copy(step, step).start()
    for step in range(steps):
        slot = step % BUFFERS
        ahead = step + BUFFERS - 1
        if ahead < steps:
            copy(ahead, ahead % BUFFERS).start()
        copy(step, slot).wait()

        def one(k, carry):
            high, low = split(held[slot, k])
            out[step * STEP + k, :B, :] = high
            out[step * STEP + k, B:, :] = low
            return carry

        lax.fori_loop(0, STEP, one, 0, unroll=4)


def rows_of(ref, start, blocks):
    return ref.at[pl.ds(start, blocks, stride=SUB), :]


def fill_table(table, value):
    high, low = split(value)
    blocks = value.shape[0]
    for start, term in enumerate((high, low, high, low)):
        rows_of(table, start, blocks)[...] = term.astype(jnp.float32)


def block_at(index):
    return pl.ds(pl.multiple_of(index * SUB, SUB), SUB)


def pair_transposed(tiles, one, two, first):
    row = jnp.where(first, one, two).astype(jnp.bfloat16)
    row = jnp.concatenate([row, row], axis=1)
    both = jnp.dot(row, tiles, preferred_element_type=jnp.float32)
    return both[:, :B], both[:, B:]


def pair_forward(tiles, one, two, first):
    zero = jnp.zeros_like(one)
    row = jnp.concatenate([jnp.where(first, one, zero), jnp.where(first, zero, two)], axis=1)
    both = lax.dot_general(
        row.astype(jnp.bfloat16),
        tiles,
        (((1,), (1,)), ((), ())),
        preferred_element_type=jnp.float32,
    )
    both = both[:, :B] + both[:, B:]
    return both, both


def over_tiles(parts, live, product, table, source, target, blocks, accs):
    places = [(accs[0], 0), (accs[0], 1), (accs[1], 2), (accs[1], 3)]
    for acc, start in places:
        rows_of(acc, start, blocks)[...] = jnp.zeros((blocks, B), jnp.float32)
    upper = lax.broadcasted_iota(jnp.int32, (SUB, B), 0) < 2
    first = 0
    for tiles in parts:
        size = tiles.shape[0]
        here = jnp.clip(live - first, 0, size)

        def some(group, carry, tiles=tiles, first=first):
            base = group * GROUP
            sums = []
            for k in range(0, GROUP, 2):
                slot = first + base + k
                pair = jnp.concatenate([tiles[base + k], tiles[base + k + 1]], axis=1)
                one, two = (table[block_at(source[slot + n]), :] for n in range(2))
                sums.append(product(pair, one, two, upper))
            for k in range(GROUP):
                slot = first + base + k
                place = block_at(jnp.where(slot < live, target[slot], blocks))
                accs[k % 2][place, :] += sums[k // 2][k % 2]
            return carry

        lax.fori_loop(0, (here + GROUP - 1) // GROUP, some, 0)
        first += size
    return sum(rows_of(acc, start, blocks)[...] for acc, start in places)


def halves(n_rows, cells):
    size = cells // n_rows
    return size, [range(core, n_rows, 2) for core in range(2)]


def adjoint_tail(n_rows, parts, pick, cell, counts, u, keep, send, table, *accs):
    fill_table(table, u)
    whole = over_tiles(parts, counts[0, 0], pair_transposed, table, pick, cell, CBLK, accs)
    square = jnp.full((TAIL, B), jnp.sum(u * u))
    size, _ = halves(n_rows, CBLK)
    core = lax.rem(lax.axis_index("rows"), 2)
    for block in range(n_rows):
        part = whole[block * size : (block + 1) * size]
        place = pl.ds(block // 2 * size, size)

        @pl.when(core == block % 2)
        def _():
            keep[place, :] = part

        @pl.when(core != block % 2)
        def _():
            send[place, :] = part

    keep[pl.ds(CBLK // 2, TAIL), :] = square
    send[pl.ds(CBLK // 2, TAIL), :] = square


def first_adjoint(n_rows, n_cols, pick, cell, counts, *rest):
    parts, pieces, (u_out, keep, send, table, *accs) = rest[:PARTS], rest[PARTS:-6], rest[-6:]
    me = lax.axis_index("cols")
    offset = 0
    for piece in pieces:
        rows = PBLK // n_cols
        for at in range(piece.shape[0] // rows):
            owner = jnp.bitwise_xor(me, offset)
            u_out[pl.ds(pl.multiple_of(owner * rows, rows), rows), :] = piece[pl.ds(at * rows, rows), :]
            offset += 1
    adjoint_tail(n_rows, parts, pick, cell, counts, u_out[...], keep, send, table, *accs)


def next_adjoint(last, n_rows, pick, cell, counts, *rest):
    parts = rest[:PARTS]
    mine, other, u_old, beta_old, *rest = rest[PARTS:]
    u_out = None if last else rest.pop(0)
    alpha_out, keep, send, table, *accs = rest
    total = mine[...] + other[...]
    alpha = jnp.sqrt(total[PBLK:])
    alpha_out[...] = alpha
    u = total[:PBLK] / alpha[:1] - alpha[:1] * (u_old[...] / beta_old[:1])
    if not last:
        u_out[...] = u
    adjoint_tail(n_rows, parts, pick, cell, counts, u, keep, send, table, *accs)


def cell_vector(n_rows, mine, other, v_old, alpha_old, v_out, beta_out, own_out):
    size, _ = halves(n_rows, CBLK)
    me = lax.axis_index("rows")
    core = lax.rem(me, 2)
    beta = jnp.sqrt(mine[pl.ds(CBLK // 2, TAIL), :])
    beta_out[...] = beta
    for block in range(n_rows):
        place = pl.ds(block // 2 * size, size)
        part = jnp.where(core == block % 2, mine[place, :], other[place, :]) / beta[:1]
        here = pl.ds(block * size, size)
        if v_old is not None:
            part = part - beta[:1] * (v_old[here, :] / alpha_old[:1])
        v_out[here, :] = part
    own_out[...] = v_out[pl.ds(pl.multiple_of(me * size, size), size), :]
    v = v_out[...]
    return v, jnp.full((TAIL, B), jnp.sum(v * v))


def forward(first, n_rows, pick, cell, counts, *rest):
    parts, rest = rest[:PARTS], rest[PARTS:]
    old = (None, None) if first else rest[2:4]
    v_out, beta_out, own_out, out, table, *accs = rest[-7:]
    v, square = cell_vector(n_rows, rest[0], rest[1], *old, v_out, beta_out, own_out)
    fill_table(table, v)
    out[:PBLK, :] = over_tiles(parts, counts[0, 0], pair_forward, table, cell, pick, PBLK, accs)
    out[pl.ds(PBLK, TAIL), :] = square


def last_vector(n_rows, mine, other, v_old, alpha_old, beta_out, own_out, square_out, v):
    _, square_out[...] = cell_vector(n_rows, mine, other, v_old, alpha_old, v, beta_out, own_out)


def finish(*refs):
    blocks, refs = refs[: ITERS + 1], refs[ITERS + 1 :]
    betas, refs = refs[: ITERS + 1], refs[ITERS + 1 :]
    alphas, refs = refs[:ITERS], refs[ITERS:]
    squares, (model_out, search_out) = refs[:-2], refs[-2:]
    betas = [ref[:1] for ref in betas]
    alphas = [ref[:1] for ref in alphas] + [jnp.sqrt(sum(ref[:1] for ref in squares))]
    phibar, rhobar = betas[0], alphas[0]
    search = blocks[0][...] / alphas[0]
    model = jnp.zeros_like(search)
    for step in range(ITERS):
        beta, alpha = betas[step + 1], alphas[step + 1]
        rho = jnp.sqrt(rhobar * rhobar + beta * beta)
        cosine = rhobar / rho
        sine = beta / rho
        theta = sine * alpha
        rhobar = -cosine * alpha
        phi = cosine * phibar
        phibar = sine * phibar
        model = model + phi / rho * search
        search = blocks[step + 1][...] / alpha - theta / rho * search
    model_out[...] = model
    search_out[...] = search


def swapped(block, axis, size, bit):
    return lax.ppermute(block, axis, [(i, i ^ bit) for i in range(size)])


def shape(*dims):
    return jax.ShapeDtypeStruct(dims, jnp.float32)


VECTOR = pl.BlockSpec(memory_space=pltpu.VMEM)
SCALAR = pl.BlockSpec(memory_space=pltpu.SMEM)


def call(kernel, outs, sources, targets, scalars, arrays):
    return pl.pallas_call(
        kernel,
        out_shape=outs,
        in_specs=[SCALAR] * len(scalars) + [VECTOR] * len(arrays),
        out_specs=[VECTOR] * len(outs),
        scratch_shapes=[
            pltpu.VMEM((sources * SUB, B), jnp.float32),
            pltpu.VMEM(((targets + 1) * SUB, B), jnp.float32),
            pltpu.VMEM(((targets + 1) * SUB, B), jnp.float32),
        ],
        compiler_params=pltpu.CompilerParams(vmem_limit_bytes=24 << 20),
    )(*scalars, *arrays)


def split_part(kernels, data, part):
    size = kernels.shape[0] // PARTS
    return pl.pallas_call(
        functools.partial(split_tiles, part * size),
        out_shape=[pltpu.VMEM((size, 2 * B, B), jnp.bfloat16), shape(*data.shape)],
        in_specs=[pl.BlockSpec(memory_space=pl.ANY), VECTOR],
        out_specs=[VECTOR, VECTOR],
        scratch_shapes=[
            pltpu.VMEM((BUFFERS, STEP, B, B), jnp.float32),
            pltpu.SemaphoreType.DMA((BUFFERS,)),
        ],
        cost_estimate=pl.CostEstimate(
            flops=4 * size * B * B, bytes_accessed=4 * size * B * B, transcendentals=0
        ),
        compiler_params=pltpu.CompilerParams(vmem_limit_bytes=24 << 20),
    )(kernels, data)


def simple_call(kernel, outs, arrays, scratch=()):
    return pl.pallas_call(
        kernel,
        out_shape=outs,
        in_specs=[VECTOR] * len(arrays),
        out_specs=[VECTOR] * len(outs),
        scratch_shapes=scratch,
        compiler_params=pltpu.CompilerParams(vmem_limit_bytes=4 << 20),
    )(*arrays)


def per_device(n_rows, n_cols, kernels, pick_index, cell_index, counts, data):
    scalars = (pick_index, cell_index, counts)
    half = CBLK // 2 + TAIL
    own = CBLK // n_rows

    def sum_cells(keep, send):
        mine = keep + swapped(send, "rows", n_rows, 1)
        bit = 2
        while bit < n_rows:
            mine = mine + swapped(mine, "rows", n_rows, bit)
            bit *= 2
        return [mine, swapped(mine, "rows", n_rows, 1)]

    partner = swapped(data, "cols", n_cols, 1)
    tiles = [None] * PARTS
    tiles[0], passed = split_part(kernels, data, 0)
    for part in range(1, PARTS):
        tiles[part], _ = split_part(kernels, data, part)
    pair = jnp.concatenate([passed, partner], axis=0)
    pieces = [pair] + [swapped(pair, "cols", n_cols, bit) for bit in range(2, n_cols, 2)]
    upick, keep, send = call(
        functools.partial(first_adjoint, n_rows, n_cols),
        [shape(PBLK, B), shape(half, B), shape(half, B)],
        PBLK,
        CBLK,
        scalars,
        tiles + pieces,
    )
    old = []
    blocks, alphas, betas = [], [], []
    for step in range(ITERS):
        vcell, beta, block, product = call(
            functools.partial(forward, step == 0, n_rows),
            [shape(CBLK, B), shape(TAIL, B), shape(own, B), shape(PBLK + TAIL, B)],
            CBLK,
            PBLK,
            scalars,
            tiles + sum_cells(keep, send) + old,
        )
        blocks.append(block)
        betas.append(beta)
        bit = 1
        while 2 * bit < n_cols:
            product = product + swapped(product, "cols", n_cols, bit)
            bit *= 2
        last = step == ITERS - 1
        *passed, alpha, keep, send = call(
            functools.partial(next_adjoint, last, n_rows),
            [shape(PBLK, B)] * (not last) + [shape(TAIL, B), shape(half, B), shape(half, B)],
            PBLK,
            CBLK,
            scalars,
            tiles + [product, swapped(product, "cols", n_cols, bit), upick, beta],
        )
        upick = passed[0] if passed else None
        alphas.append(alpha)
        old = [vcell, alpha]
    beta, block, square = simple_call(
        functools.partial(last_vector, n_rows),
        [shape(TAIL, B), shape(own, B), shape(TAIL, B)],
        sum_cells(keep, send) + old,
        [pltpu.VMEM((CBLK, B), jnp.float32)],
    )
    blocks.append(block)
    betas.append(beta)
    square = square + swapped(square, "cols", n_cols, 1)
    squares = [square] + [swapped(square, "cols", n_cols, bit) for bit in range(2, n_cols, 2)]
    model, search = simple_call(
        finish, [shape(own, B), shape(own, B)], blocks + betas + alphas + squares
    )
    return (model, search)


def solution(mesh):
    def run(*args):
        return per_device(mesh.shape["rows"], mesh.shape["cols"], *args)

    return jax.shard_map(
        run,
        mesh=mesh,
        in_specs=(
            P(("rows", "cols"), None, None),
            P(("rows", "cols")),
            P(("rows", "cols")),
            P("rows", "cols"),
            P("cols", "rows"),
        ),
        out_specs=(P("rows", "cols"), P("rows", "cols")),
        check_vma=False,
    )
```

```python
import functools

import jax
import jax.numpy as jnp
from jax import lax
from jax.experimental import pallas as pl
from jax.experimental.pallas import tpu as pltpu
from jax.sharding import PartitionSpec as P

PBLK = 128
CBLK = 512
ITERS = 2
B = 128
SUB = 8
GROUP = 80
PARTS = 2
STEP = 32
BUFFERS = 3
TAIL = 8


def split(value):
    high = value.astype(jnp.bfloat16)
    return high, (value - high.astype(jnp.float32)).astype(jnp.bfloat16)


def split_tiles(start, tiles, data, out, data_out, held, arrived):
    steps = out.shape[0] // STEP
    data_out[...] = data[...]

    def copy(step, slot):
        return pltpu.make_async_copy(
            tiles.at[pl.ds(start + step * STEP, STEP)], held.at[slot], arrived.at[slot]
        )

    for step in range(min(BUFFERS - 1, steps)):
        copy(step, step).start()
    for step in range(steps):
        slot = step % BUFFERS
        ahead = step + BUFFERS - 1
        if ahead < steps:
            copy(ahead, ahead % BUFFERS).start()
        copy(step, slot).wait()

        def one(k, carry):
            high, low = split(held[slot, k])
            out[step * STEP + k, :B, :] = high
            out[step * STEP + k, B:, :] = low
            return carry

        lax.fori_loop(0, STEP, one, 0, unroll=4)


def fill_table(table, value):
    for index, term in enumerate(split(value)):
        table[index] = term.astype(jnp.float32)


def row_pair(table, source, slot, forward, at):
    place = lax.broadcasted_iota(jnp.int32, (SUB, B), 0)

    def term(n, index):
        row = jnp.broadcast_to(table[index, pl.ds(source[slot + n], 1), :], (SUB, B))
        return jnp.where(place == at + n, row, 0.0)

    def both(*tiles):
        terms = [sum(term(n, index) for n in tiles) for index in range(2)]
        return jnp.concatenate(terms, axis=0).astype(jnp.bfloat16)

    if forward:
        return jnp.concatenate([both(0), both(1)], axis=1)
    return jnp.concatenate([both(0, 1)] * 2, axis=1)


def eight(tiles, base, table, source, slot, forward):
    total = jnp.zeros((2 * SUB, 2 * B), jnp.float32)
    over = ((1,), (1 if forward else 0,))
    for k in range(0, SUB, 2):
        pair = jnp.concatenate([tiles[base + k], tiles[base + k + 1]], axis=1)
        row = row_pair(table, source, slot + k, forward, k)
        total += lax.dot_general(row, pair, (over, ((), ())), preferred_element_type=jnp.float32)
    total = total[:SUB] + total[SUB:]
    if forward:
        return total[:, :B] + total[:, B:]
    odd = lax.rem(lax.broadcasted_iota(jnp.int32, (SUB, B), 0), 2) == 1
    return jnp.where(odd, total[:, B:], total[:, :B])


def over_tiles(parts, live, forward, table, source, targets, blocks, sums):
    sums[...] = jnp.zeros_like(sums)
    first = 0
    for tiles in parts:
        size = tiles.shape[0]
        here = jnp.clip(live - first, 0, size)

        def some(group, carry, tiles=tiles, first=first):
            for k in range(0, GROUP, SUB):
                base = group * GROUP + k
                slot = first + base
                value = eight(tiles, base, table, source, slot, forward)
                sums[pl.ds(pl.multiple_of(slot, SUB), SUB), :] = value
            return carry

        lax.fori_loop(0, (here + GROUP - 1) // GROUP, some, 0)
        first += size
    slots = sums.shape[0]
    block = lax.broadcasted_iota(jnp.int32, (blocks, slots), 0)
    slot = lax.broadcasted_iota(jnp.int32, (1, slots), 1)
    chosen = block == jnp.where(slot < live, targets[...], -1)
    chosen = jnp.where(chosen, 1.0, 0.0).astype(jnp.bfloat16)
    both = jnp.concatenate(split(sums[...]), axis=1)
    total = jnp.dot(chosen, both, preferred_element_type=jnp.float32)
    return total[:, :B] + total[:, B:]


def halves(n_rows, cells):
    size = cells // n_rows
    return size, [range(core, n_rows, 2) for core in range(2)]


def adjoint_tail(n_rows, parts, pick, cells, counts, u, keep, send, table, sums):
    fill_table(table, u)
    whole = over_tiles(parts, counts[0, 0], False, table, pick, cells, CBLK, sums)
    square = jnp.full((TAIL, B), jnp.sum(u * u))
    size, _ = halves(n_rows, CBLK)
    core = lax.rem(lax.axis_index("rows"), 2)
    for block in range(n_rows):
        part = whole[block * size : (block + 1) * size]
        place = pl.ds(block // 2 * size, size)

        @pl.when(core == block % 2)
        def _():
            keep[place, :] = part

        @pl.when(core != block % 2)
        def _():
            send[place, :] = part

    keep[pl.ds(CBLK // 2, TAIL), :] = square
    send[pl.ds(CBLK // 2, TAIL), :] = square


def first_adjoint(n_rows, n_cols, pick, counts, cells, *rest):
    parts, pieces, (u_out, keep, send, table, sums) = rest[:PARTS], rest[PARTS:-5], rest[-5:]
    me = lax.axis_index("cols")
    offset = 0
    for piece in pieces:
        rows = PBLK // n_cols
        for at in range(piece.shape[0] // rows):
            owner = jnp.bitwise_xor(me, offset)
            u_out[pl.ds(pl.multiple_of(owner * rows, rows), rows), :] = piece[pl.ds(at * rows, rows), :]
            offset += 1
    adjoint_tail(n_rows, parts, pick, cells, counts, u_out[...], keep, send, table, sums)


def next_adjoint(last, n_rows, pick, counts, cells, *rest):
    parts = rest[:PARTS]
    mine, other, u_old, beta_old, *rest = rest[PARTS:]
    u_out = None if last else rest.pop(0)
    alpha_out, keep, send, table, sums = rest
    total = mine[...] + other[...]
    alpha = jnp.sqrt(total[PBLK:])
    alpha_out[...] = alpha
    u = total[:PBLK] / alpha[:1] - alpha[:1] * (u_old[...] / beta_old[:1])
    if not last:
        u_out[...] = u
    adjoint_tail(n_rows, parts, pick, cells, counts, u, keep, send, table, sums)


def cell_vector(n_rows, mine, other, v_old, alpha_old, v_out, beta_out, own_out):
    size, _ = halves(n_rows, CBLK)
    me = lax.axis_index("rows")
    core = lax.rem(me, 2)
    beta = jnp.sqrt(mine[pl.ds(CBLK // 2, TAIL), :])
    beta_out[...] = beta
    for block in range(n_rows):
        place = pl.ds(block // 2 * size, size)
        part = jnp.where(core == block % 2, mine[place, :], other[place, :]) / beta[:1]
        here = pl.ds(block * size, size)
        if v_old is not None:
            part = part - beta[:1] * (v_old[here, :] / alpha_old[:1])
        v_out[here, :] = part
    own_out[...] = v_out[pl.ds(pl.multiple_of(me * size, size), size), :]
    v = v_out[...]
    return v, jnp.full((TAIL, B), jnp.sum(v * v))


def forward(first, n_rows, cell, counts, picks, *rest):
    parts, rest = rest[:PARTS], rest[PARTS:]
    old = (None, None) if first else rest[2:4]
    v_out, beta_out, own_out, out, table, sums = rest[-6:]
    v, square = cell_vector(n_rows, rest[0], rest[1], *old, v_out, beta_out, own_out)
    fill_table(table, v)
    out[:PBLK, :] = over_tiles(parts, counts[0, 0], True, table, cell, picks, PBLK, sums)
    out[pl.ds(PBLK, TAIL), :] = square


def last_vector(n_rows, mine, other, v_old, alpha_old, beta_out, own_out, square_out, v):
    _, square_out[...] = cell_vector(n_rows, mine, other, v_old, alpha_old, v, beta_out, own_out)


def finish(*refs):
    blocks, refs = refs[: ITERS + 1], refs[ITERS + 1 :]
    betas, refs = refs[: ITERS + 1], refs[ITERS + 1 :]
    alphas, refs = refs[:ITERS], refs[ITERS:]
    squares, (model_out, search_out) = refs[:-2], refs[-2:]
    betas = [ref[:1] for ref in betas]
    alphas = [ref[:1] for ref in alphas] + [jnp.sqrt(sum(ref[:1] for ref in squares))]
    phibar, rhobar = betas[0], alphas[0]
    search = blocks[0][...] / alphas[0]
    model = jnp.zeros_like(search)
    for step in range(ITERS):
        beta, alpha = betas[step + 1], alphas[step + 1]
        rho = jnp.sqrt(rhobar * rhobar + beta * beta)
        cosine = rhobar / rho
        sine = beta / rho
        theta = sine * alpha
        rhobar = -cosine * alpha
        phi = cosine * phibar
        phibar = sine * phibar
        model = model + phi / rho * search
        search = blocks[step + 1][...] / alpha - theta / rho * search
    model_out[...] = model
    search_out[...] = search


def swapped(block, axis, size, bit):
    return lax.ppermute(block, axis, [(i, i ^ bit) for i in range(size)])


def shape(*dims):
    return jax.ShapeDtypeStruct(dims, jnp.float32)


VECTOR = pl.BlockSpec(memory_space=pltpu.VMEM)
SCALAR = pl.BlockSpec(memory_space=pltpu.SMEM)


def call(kernel, outs, blocks, source, counts, targets, tiles, arrays):
    slots = targets.shape[1]
    return pl.pallas_call(
        kernel,
        out_shape=outs,
        in_specs=[SCALAR] * 2 + [VECTOR] * (1 + len(tiles) + len(arrays)),
        out_specs=[VECTOR] * len(outs),
        scratch_shapes=[
            pltpu.VMEM((2, blocks, B), jnp.float32),
            pltpu.VMEM((slots, B), jnp.float32),
        ],
        compiler_params=pltpu.CompilerParams(vmem_limit_bytes=16 << 20),
    )(source, counts, targets, *tiles, *arrays)


def split_part(kernels, data, part):
    size = kernels.shape[0] // PARTS
    return pl.pallas_call(
        functools.partial(split_tiles, part * size),
        out_shape=[pltpu.VMEM((size, 2 * B, B), jnp.bfloat16), shape(*data.shape)],
        in_specs=[pl.BlockSpec(memory_space=pl.ANY), VECTOR],
        out_specs=[VECTOR, VECTOR],
        scratch_shapes=[
            pltpu.VMEM((BUFFERS, STEP, B, B), jnp.float32),
            pltpu.SemaphoreType.DMA((BUFFERS,)),
        ],
        cost_estimate=pl.CostEstimate(
            flops=4 * size * B * B, bytes_accessed=4 * size * B * B, transcendentals=0
        ),
        compiler_params=pltpu.CompilerParams(vmem_limit_bytes=24 << 20),
    )(kernels, data)


def simple_call(kernel, outs, arrays, scratch=()):
    return pl.pallas_call(
        kernel,
        out_shape=outs,
        in_specs=[VECTOR] * len(arrays),
        out_specs=[VECTOR] * len(outs),
        scratch_shapes=scratch,
        compiler_params=pltpu.CompilerParams(vmem_limit_bytes=4 << 20),
    )(*arrays)


def per_device(n_rows, n_cols, kernels, pick_index, cell_index, counts, data):
    slots = kernels.shape[0]
    by_pick = (pick_index, counts, cell_index.reshape(1, slots))
    by_cell = (cell_index, counts, pick_index.reshape(1, slots))
    half = CBLK // 2 + TAIL
    own = CBLK // n_rows

    def sum_cells(keep, send):
        mine = keep + swapped(send, "rows", n_rows, 1)
        bit = 2
        while bit < n_rows:
            mine = mine + swapped(mine, "rows", n_rows, bit)
            bit *= 2
        return [mine, swapped(mine, "rows", n_rows, 1)]

    partner = swapped(data, "cols", n_cols, 1)
    tiles = [None] * PARTS
    tiles[0], passed = split_part(kernels, data, 0)
    for part in range(1, PARTS):
        tiles[part], _ = split_part(kernels, data, part)
    pair = jnp.concatenate([passed, partner], axis=0)
    pieces = [pair] + [swapped(pair, "cols", n_cols, bit) for bit in range(2, n_cols, 2)]
    upick, keep, send = call(
        functools.partial(first_adjoint, n_rows, n_cols),
        [shape(PBLK, B), shape(half, B), shape(half, B)],
        PBLK,
        *by_pick,
        tiles,
        pieces,
    )
    old = []
    blocks, alphas, betas = [], [], []
    for step in range(ITERS):
        vcell, beta, block, product = call(
            functools.partial(forward, step == 0, n_rows),
            [shape(CBLK, B), shape(TAIL, B), shape(own, B), shape(PBLK + TAIL, B)],
            CBLK,
            *by_cell,
            tiles,
            sum_cells(keep, send) + old,
        )
        blocks.append(block)
        betas.append(beta)
        bit = 1
        while 2 * bit < n_cols:
            product = product + swapped(product, "cols", n_cols, bit)
            bit *= 2
        last = step == ITERS - 1
        *passed, alpha, keep, send = call(
            functools.partial(next_adjoint, last, n_rows),
            [shape(PBLK, B)] * (not last) + [shape(TAIL, B), shape(half, B), shape(half, B)],
            PBLK,
            *by_pick,
            tiles,
            [product, swapped(product, "cols", n_cols, bit), upick, beta],
        )
        upick = passed[0] if passed else None
        alphas.append(alpha)
        old = [vcell, alpha]
    beta, block, square = simple_call(
        functools.partial(last_vector, n_rows),
        [shape(TAIL, B), shape(own, B), shape(TAIL, B)],
        sum_cells(keep, send) + old,
        [pltpu.VMEM((CBLK, B), jnp.float32)],
    )
    blocks.append(block)
    betas.append(beta)
    square = square + swapped(square, "cols", n_cols, 1)
    squares = [square] + [swapped(square, "cols", n_cols, bit) for bit in range(2, n_cols, 2)]
    model, search = simple_call(
        finish, [shape(own, B), shape(own, B)], blocks + betas + alphas + squares
    )
    return (model, search)


def solution(mesh):
    def run(*args):
        return per_device(mesh.shape["rows"], mesh.shape["cols"], *args)

    return jax.shard_map(
        run,
        mesh=mesh,
        in_specs=(
            P(("rows", "cols"), None, None),
            P(("rows", "cols")),
            P(("rows", "cols")),
            P("rows", "cols"),
            P("cols", "rows"),
        ),
        out_specs=(P("rows", "cols"), P("rows", "cols")),
        check_vma=False,
    )
```

```python
import functools

import jax
import jax.numpy as jnp
from jax import lax
from jax.experimental import pallas as pl
from jax.experimental.pallas import tpu as pltpu
from jax.sharding import PartitionSpec as P

PBLK = 128
CBLK = 512
ITERS = 2
B = 128
SUB = 8
GROUP = 80
SHARES = (1, 1, 2)
PARTS = len(SHARES)
TURNED = 2
STEP = 16
BUFFERS = 4
CHUNK = 32
TAIL = 8


def split(value):
    high = value.astype(jnp.bfloat16)
    return high, (value - high.astype(jnp.float32)).astype(jnp.bfloat16)


def split_tiles(start, tiles, data, out, data_out, held, arrived, passed):
    steps = out.shape[0] // STEP
    through = pltpu.make_async_copy(data, data_out, passed)
    through.start()

    def copy(step, slot):
        return pltpu.make_async_copy(
            tiles.at[pl.ds(start + step * STEP, STEP)], held.at[slot], arrived.at[slot]
        )

    for step in range(min(BUFFERS - 1, steps)):
        copy(step, step).start()
    for step in range(steps):
        slot = step % BUFFERS
        ahead = step + BUFFERS - 1
        if ahead < steps:
            copy(ahead, ahead % BUFFERS).start()
        copy(step, slot).wait()

        def one(k, carry):
            for row in range(0, B, CHUNK):
                high, low = split(held[slot, k, pl.ds(row, CHUNK), :])
                out[step * STEP + k, pl.ds(row, CHUNK), :] = high
                out[step * STEP + k, pl.ds(B + row, CHUNK), :] = low
            return carry

        lax.fori_loop(0, STEP, one, 0, unroll=4)
    through.wait()


def turn_tiles(*refs):
    through = pltpu.make_async_copy(refs[TURNED], refs[TURNED + 1], refs[-1])
    through.start()
    for tiles, out in zip(refs[:TURNED], refs[TURNED + 2 : -1]):

        def one(k, carry, tiles=tiles, out=out):
            out[k, :B, :] = tiles[k, :B, :].T
            out[k, B:, :] = tiles[k, B:, :].T
            return carry

        lax.fori_loop(0, tiles.shape[0], one, 0, unroll=4)
    through.wait()


def fill_table(table, value):
    for index, term in enumerate(split(value)):
        table[index] = term.astype(jnp.float32)


def row_pair(table, source, slot, at, turned):
    place = lax.broadcasted_iota(jnp.int32, (SUB, B), 0)

    def term(n, index):
        row = jnp.broadcast_to(table[index, pl.ds(source[slot + n], 1), :], (SUB, B))
        return jnp.where(place == at + n, row, 0.0)

    def both(*tiles):
        terms = [sum(term(n, index) for n in tiles) for index in range(2)]
        return jnp.concatenate(terms, axis=0).astype(jnp.bfloat16)

    if turned:
        return jnp.concatenate([both(0), both(1)], axis=1)
    return jnp.concatenate([both(0, 1)] * 2, axis=1)


def eight(tiles, base, table, source, slot, turned):
    total = jnp.zeros((2 * SUB, 2 * B), jnp.float32)
    over = ((1,), (1 if turned else 0,))
    for k in range(0, SUB, 2):
        pair = jnp.concatenate([tiles[base + k], tiles[base + k + 1]], axis=1)
        row = row_pair(table, source, slot + k, k, turned)
        total += lax.dot_general(row, pair, (over, ((), ())), preferred_element_type=jnp.float32)
    total = total[:SUB] + total[SUB:]
    if turned:
        return total[:, :B] + total[:, B:]
    odd = lax.rem(lax.broadcasted_iota(jnp.int32, (SUB, B), 0), 2) == 1
    return jnp.where(odd, total[:, B:], total[:, :B])


def over_tiles(parts, live, table, source, targets, blocks, sums, turned=0):
    sums[...] = jnp.zeros_like(sums)
    first = 0
    for part, tiles in enumerate(parts):
        size = tiles.shape[0]
        turn = part >= len(parts) - turned
        here = jnp.clip(live - first, 0, size)

        def some(group, carry, tiles=tiles, first=first, turn=turn):
            for k in range(0, GROUP, SUB):
                base = group * GROUP + k
                slot = first + base
                value = eight(tiles, base, table, source, slot, turn)
                sums[pl.ds(pl.multiple_of(slot, SUB), SUB), :] = value
            return carry

        lax.fori_loop(0, (here + GROUP - 1) // GROUP, some, 0)
        first += size
    slots = sums.shape[0]
    block = lax.broadcasted_iota(jnp.int32, (blocks, slots), 0)
    slot = lax.broadcasted_iota(jnp.int32, (1, slots), 1)
    chosen = block == jnp.where(slot < live, targets[...], -1)
    chosen = jnp.where(chosen, 1.0, 0.0).astype(jnp.bfloat16)
    both = jnp.concatenate(split(sums[...]), axis=1)
    total = jnp.dot(chosen, both, preferred_element_type=jnp.float32)
    return total[:, :B] + total[:, B:]


def halves(n_rows, cells):
    size = cells // n_rows
    return size, [range(core, n_rows, 2) for core in range(2)]


def adjoint_tail(n_rows, parts, pick, cells, counts, u, keep, send, table, sums):
    fill_table(table, u)
    whole = over_tiles(parts, counts[0, 0], table, pick, cells, CBLK, sums)
    square = jnp.full((TAIL, B), jnp.sum(u * u))
    size, _ = halves(n_rows, CBLK)
    core = lax.rem(lax.axis_index("rows"), 2)
    for block in range(n_rows):
        part = whole[block * size : (block + 1) * size]
        place = pl.ds(block // 2 * size, size)

        @pl.when(core == block % 2)
        def _():
            keep[place, :] = part

        @pl.when(core != block % 2)
        def _():
            send[place, :] = part

    keep[pl.ds(CBLK // 2, TAIL), :] = square
    send[pl.ds(CBLK // 2, TAIL), :] = square


def first_adjoint(n_rows, n_cols, pick, counts, cells, *rest):
    parts, pieces, (u_out, keep, send, table, sums) = rest[:PARTS], rest[PARTS:-5], rest[-5:]
    me = lax.axis_index("cols")
    offset = 0
    for piece in pieces:
        rows = PBLK // n_cols
        for at in range(piece.shape[0] // rows):
            owner = jnp.bitwise_xor(me, offset)
            u_out[pl.ds(pl.multiple_of(owner * rows, rows), rows), :] = piece[pl.ds(at * rows, rows), :]
            offset += 1
    adjoint_tail(n_rows, parts, pick, cells, counts, u_out[...], keep, send, table, sums)


def next_adjoint(last, n_rows, pick, counts, cells, *rest):
    parts = rest[:PARTS]
    mine, other, u_old, beta_old, *rest = rest[PARTS:]
    u_out = None if last else rest.pop(0)
    alpha_out, keep, send, table, sums = rest
    total = mine[...] + other[...]
    alpha = jnp.sqrt(total[PBLK:])
    alpha_out[...] = alpha
    u = total[:PBLK] / alpha[:1] - alpha[:1] * (u_old[...] / beta_old[:1])
    if not last:
        u_out[...] = u
    adjoint_tail(n_rows, parts, pick, cells, counts, u, keep, send, table, sums)


def cell_vector(n_rows, mine, other, v_old, alpha_old, v_out, beta_out, own_out):
    size, _ = halves(n_rows, CBLK)
    me = lax.axis_index("rows")
    core = lax.rem(me, 2)
    beta = jnp.sqrt(mine[pl.ds(CBLK // 2, TAIL), :])
    beta_out[...] = beta
    for block in range(n_rows):
        place = pl.ds(block // 2 * size, size)
        part = jnp.where(core == block % 2, mine[place, :], other[place, :]) / beta[:1]
        here = pl.ds(block * size, size)
        if v_old is not None:
            part = part - beta[:1] * (v_old[here, :] / alpha_old[:1])
        v_out[here, :] = part
    own_out[...] = v_out[pl.ds(pl.multiple_of(me * size, size), size), :]
    v = v_out[...]
    return v, jnp.full((TAIL, B), jnp.sum(v * v))


def forward(first, n_rows, cell, counts, picks, *rest):
    parts, rest = rest[:PARTS], rest[PARTS:]
    old = (None, None) if first else rest[2:4]
    v_out, beta_out, own_out, out, table, sums = rest[-6:]
    v, square = cell_vector(n_rows, rest[0], rest[1], *old, v_out, beta_out, own_out)
    fill_table(table, v)
    out[:PBLK, :] = over_tiles(parts, counts[0, 0], table, cell, picks, PBLK, sums, PARTS - TURNED)
    out[pl.ds(PBLK, TAIL), :] = square


def last_vector(n_rows, mine, other, v_old, alpha_old, beta_out, own_out, square_out, v):
    _, square_out[...] = cell_vector(n_rows, mine, other, v_old, alpha_old, v, beta_out, own_out)


def finish(*refs):
    blocks, refs = refs[: ITERS + 1], refs[ITERS + 1 :]
    betas, refs = refs[: ITERS + 1], refs[ITERS + 1 :]
    alphas, refs = refs[:ITERS], refs[ITERS:]
    squares, (model_out, search_out) = refs[:-2], refs[-2:]
    betas = [ref[:1] for ref in betas]
    alphas = [ref[:1] for ref in alphas] + [jnp.sqrt(sum(ref[:1] for ref in squares))]
    phibar, rhobar = betas[0], alphas[0]
    search = blocks[0][...] / alphas[0]
    model = jnp.zeros_like(search)
    for step in range(ITERS):
        beta, alpha = betas[step + 1], alphas[step + 1]
        rho = jnp.sqrt(rhobar * rhobar + beta * beta)
        cosine = rhobar / rho
        sine = beta / rho
        theta = sine * alpha
        rhobar = -cosine * alpha
        phi = cosine * phibar
        phibar = sine * phibar
        model = model + phi / rho * search
        search = blocks[step + 1][...] / alpha - theta / rho * search
    model_out[...] = model
    search_out[...] = search


def swapped(block, axis, size, bit):
    return lax.ppermute(block, axis, [(i, i ^ bit) for i in range(size)])


def shape(*dims):
    return jax.ShapeDtypeStruct(dims, jnp.float32)


VECTOR = pl.BlockSpec(memory_space=pltpu.VMEM)
SCALAR = pl.BlockSpec(memory_space=pltpu.SMEM)


def call(kernel, outs, blocks, source, counts, targets, tiles, arrays):
    slots = targets.shape[1]
    return pl.pallas_call(
        kernel,
        out_shape=outs,
        in_specs=[SCALAR] * 2 + [VECTOR] * (1 + len(tiles) + len(arrays)),
        out_specs=[VECTOR] * len(outs),
        scratch_shapes=[
            pltpu.VMEM((2, blocks, B), jnp.float32),
            pltpu.VMEM((slots, B), jnp.float32),
        ],
        compiler_params=pltpu.CompilerParams(vmem_limit_bytes=12 << 20),
    )(source, counts, targets, *tiles, *arrays)


def split_part(kernels, data, start, size):
    if start == 0:
        data = pltpu.with_memory_space_constraint(data, pltpu.HBM)
    return pl.pallas_call(
        functools.partial(split_tiles, start),
        out_shape=[pltpu.VMEM((size, 2 * B, B), jnp.bfloat16), shape(*data.shape)],
        in_specs=[pl.BlockSpec(memory_space=pltpu.HBM), pl.BlockSpec(memory_space=pl.ANY)],
        out_specs=[VECTOR, VECTOR],
        scratch_shapes=[
            pltpu.VMEM((BUFFERS, STEP, B, B), jnp.float32),
            pltpu.SemaphoreType.DMA((BUFFERS,)),
            pltpu.SemaphoreType.DMA,
        ],
        cost_estimate=pl.CostEstimate(
            flops=4 * size * B * B, bytes_accessed=4 * size * B * B, transcendentals=0
        ),
        compiler_params=pltpu.CompilerParams(vmem_limit_bytes=12 << 20),
    )(kernels, data)


def turned(tiles, data):
    total = sum(part.shape[0] for part in tiles)
    data, *out = pl.pallas_call(
        turn_tiles,
        out_shape=[shape(*data.shape)] + [pltpu.VMEM(part.shape, part.dtype) for part in tiles],
        in_specs=[VECTOR] * TURNED + [pl.BlockSpec(memory_space=pl.ANY)],
        out_specs=[VECTOR] * (TURNED + 1),
        scratch_shapes=[pltpu.SemaphoreType.DMA],
        cost_estimate=pl.CostEstimate(
            flops=0, bytes_accessed=2 * total * B * B, transcendentals=0
        ),
        compiler_params=pltpu.CompilerParams(vmem_limit_bytes=4 << 20),
    )(*tiles, data)
    return data, out


def simple_call(kernel, outs, arrays, scratch=()):
    return pl.pallas_call(
        kernel,
        out_shape=outs,
        in_specs=[VECTOR] * len(arrays),
        out_specs=[VECTOR] * len(outs),
        scratch_shapes=scratch,
        compiler_params=pltpu.CompilerParams(vmem_limit_bytes=4 << 20),
    )(*arrays)


def per_device(n_rows, n_cols, kernels, pick_index, cell_index, counts, data):
    slots = kernels.shape[0]
    by_pick = (pick_index, counts, cell_index.reshape(1, slots))
    by_cell = (cell_index, counts, pick_index.reshape(1, slots))
    half = CBLK // 2 + TAIL
    own = CBLK // n_rows

    transposed = []

    def sum_cells(keep, send):
        mine = keep + swapped(send, "rows", n_rows, 1)
        bit = 2
        while bit < n_rows:
            other = swapped(mine, "rows", n_rows, bit)
            if not transposed:
                mine, parts = turned(tiles[:TURNED], mine)
                transposed.extend(parts + tiles[TURNED:])
            mine = mine + other
            bit *= 2
        return [mine, swapped(mine, "rows", n_rows, 1)]

    kernels = pltpu.with_memory_space_constraint(kernels, pltpu.HBM)
    tiles = []
    held = data
    partner = None
    bit = 1
    for share in SHARES:
        if bit < n_cols:
            held = held if partner is None else jnp.concatenate([held, partner], axis=0)
            partner = swapped(held, "cols", n_cols, bit)
            bit *= 2
        start = sum(part.shape[0] for part in tiles)
        part, passed = split_part(kernels, held, start, slots * share // sum(SHARES))
        tiles.append(part)
        if bit < n_cols:
            held = passed
    while bit < n_cols:
        held = jnp.concatenate([held, partner], axis=0)
        partner = swapped(held, "cols", n_cols, bit)
        bit *= 2
    pieces = [held, partner]
    upick, keep, send = call(
        functools.partial(first_adjoint, n_rows, n_cols),
        [shape(PBLK, B), shape(half, B), shape(half, B)],
        PBLK,
        *by_pick,
        tiles,
        pieces,
    )
    old = []
    blocks, alphas, betas = [], [], []
    for step in range(ITERS):
        sums = sum_cells(keep, send)
        vcell, beta, block, product = call(
            functools.partial(forward, step == 0, n_rows),
            [shape(CBLK, B), shape(TAIL, B), shape(own, B), shape(PBLK + TAIL, B)],
            CBLK,
            *by_cell,
            transposed,
            sums + old,
        )
        blocks.append(block)
        betas.append(beta)
        bit = 1
        while 2 * bit < n_cols:
            product = product + swapped(product, "cols", n_cols, bit)
            bit *= 2
        last = step == ITERS - 1
        *passed, alpha, keep, send = call(
            functools.partial(next_adjoint, last, n_rows),
            [shape(PBLK, B)] * (not last) + [shape(TAIL, B), shape(half, B), shape(half, B)],
            PBLK,
            *by_pick,
            tiles,
            [product, swapped(product, "cols", n_cols, bit), upick, beta],
        )
        upick = passed[0] if passed else None
        alphas.append(alpha)
        old = [vcell, alpha]
    beta, block, square = simple_call(
        functools.partial(last_vector, n_rows),
        [shape(TAIL, B), shape(own, B), shape(TAIL, B)],
        sum_cells(keep, send) + old,
        [pltpu.VMEM((CBLK, B), jnp.float32)],
    )
    blocks.append(block)
    betas.append(beta)
    square = square + swapped(square, "cols", n_cols, 1)
    squares = [square] + [swapped(square, "cols", n_cols, bit) for bit in range(2, n_cols, 2)]
    model, search = simple_call(
        finish, [shape(own, B), shape(own, B)], blocks + betas + alphas + squares
    )
    return (model, search)


def solution(mesh):
    def run(*args):
        return per_device(mesh.shape["rows"], mesh.shape["cols"], *args)

    return jax.shard_map(
        run,
        mesh=mesh,
        in_specs=(
            P(("rows", "cols"), None, None),
            P(("rows", "cols")),
            P(("rows", "cols")),
            P("rows", "cols"),
            P("cols", "rows"),
        ),
        out_specs=(P("rows", "cols"), P("rows", "cols")),
        check_vma=False,
    )
```

```python
import functools

import jax
import jax.numpy as jnp
from jax import lax
from jax.experimental import pallas as pl
from jax.experimental.pallas import tpu as pltpu
from jax.sharding import PartitionSpec as P

PBLK = 128
CBLK = 512
ITERS = 2
B = 128
SUB = 8
GROUP = 80
SHARES = (1, 1, 2)
PARTS = len(SHARES)
TURNED = 2
STEP = 16
BUFFERS = 4
CHUNK = 32
TAIL = 8


def split(value):
    high = value.astype(jnp.bfloat16)
    return high, (value - high.astype(jnp.float32)).astype(jnp.bfloat16)


def split_tiles(start, passes, tiles, *rest):
    if passes:
        data, out, data_out, held, arrived, passed = rest
        through = pltpu.make_async_copy(data, data_out, passed)
        through.start()
    else:
        out, held, arrived = rest
    steps = out.shape[0] // STEP

    def copy(step):
        slot = lax.rem(step, BUFFERS)
        return pltpu.make_async_copy(
            tiles.at[pl.ds(start + step * STEP, STEP)], held.at[slot], arrived.at[slot]
        )

    for step in range(min(BUFFERS - 1, steps)):
        copy(jnp.int32(step)).start()

    def one(step, carry):
        @pl.when(step + BUFFERS - 1 < steps)
        def _():
            copy(step + BUFFERS - 1).start()

        copy(step).wait()
        slot = lax.rem(step, BUFFERS)
        for k in range(STEP):
            for row in range(0, B, CHUNK):
                high, low = split(held[slot, k, pl.ds(row, CHUNK), :])
                out[step * STEP + k, pl.ds(row, CHUNK), :] = high
                out[step * STEP + k, pl.ds(B + row, CHUNK), :] = low
        return carry

    lax.fori_loop(0, steps, one, 0)
    if passes:
        through.wait()


def turn_tiles(*refs):
    through = pltpu.make_async_copy(refs[TURNED], refs[TURNED + 1], refs[-1])
    through.start()
    for tiles, out in zip(refs[:TURNED], refs[TURNED + 2 : -1]):

        def one(k, carry, tiles=tiles, out=out):
            out[k, :B, :] = tiles[k, :B, :].T
            out[k, B:, :] = tiles[k, B:, :].T
            return carry

        lax.fori_loop(0, tiles.shape[0], one, 0, unroll=8)
    through.wait()


def fill_table(table, value):
    for index, term in enumerate(split(value)):
        table[index] = term.astype(jnp.float32)


def row_pair(table, source, slot, at, turned):
    place = lax.broadcasted_iota(jnp.int32, (SUB, B), 0)

    def term(n, index):
        row = jnp.broadcast_to(table[index, pl.ds(source[slot + n], 1), :], (SUB, B))
        return jnp.where(place == at + n, row, 0.0)

    def both(*tiles):
        terms = [sum(term(n, index) for n in tiles) for index in range(2)]
        return jnp.concatenate(terms, axis=0).astype(jnp.bfloat16)

    if turned:
        return jnp.concatenate([both(0), both(1)], axis=1)
    return jnp.concatenate([both(0, 1)] * 2, axis=1)


def eight(tiles, base, table, source, slot, turned):
    total = jnp.zeros((2 * SUB, 2 * B), jnp.float32)
    over = ((1,), (1 if turned else 0,))
    for k in range(0, SUB, 2):
        pair = jnp.concatenate([tiles[base + k], tiles[base + k + 1]], axis=1)
        row = row_pair(table, source, slot + k, k, turned)
        total += lax.dot_general(row, pair, (over, ((), ())), preferred_element_type=jnp.float32)
    total = total[:SUB] + total[SUB:]
    if turned:
        return total[:, :B] + total[:, B:]
    odd = lax.rem(lax.broadcasted_iota(jnp.int32, (SUB, B), 0), 2) == 1
    return jnp.where(odd, total[:, B:], total[:, :B])


def over_tiles(parts, live, table, source, targets, blocks, sums, turned=0):
    sums[...] = jnp.zeros_like(sums)
    first = 0
    for part, tiles in enumerate(parts):
        size = tiles.shape[0]
        turn = part >= len(parts) - turned
        here = jnp.clip(live - first, 0, size)

        def some(group, carry, tiles=tiles, first=first, turn=turn):
            for k in range(0, GROUP, SUB):
                base = group * GROUP + k
                slot = first + base
                value = eight(tiles, base, table, source, slot, turn)
                sums[pl.ds(pl.multiple_of(slot, SUB), SUB), :] = value
            return carry

        lax.fori_loop(0, (here + GROUP - 1) // GROUP, some, 0)
        first += size
    slots = sums.shape[0]
    block = lax.broadcasted_iota(jnp.int32, (blocks, slots), 0)
    slot = lax.broadcasted_iota(jnp.int32, (1, slots), 1)
    chosen = block == jnp.where(slot < live, targets[...], -1)
    chosen = jnp.where(chosen, 1.0, 0.0).astype(jnp.bfloat16)
    both = jnp.concatenate(split(sums[...]), axis=1)
    total = jnp.dot(chosen, both, preferred_element_type=jnp.float32)
    return total[:, :B] + total[:, B:]


def halves(n_rows, cells):
    size = cells // n_rows
    return size, [range(core, n_rows, 2) for core in range(2)]


def adjoint_tail(n_rows, parts, pick, cells, counts, u, keep, send, table, sums):
    fill_table(table, u)
    whole = over_tiles(parts, counts[0, 0], table, pick, cells, CBLK, sums)
    square = jnp.full((TAIL, B), jnp.sum(u * u))
    size, _ = halves(n_rows, CBLK)
    core = lax.rem(lax.axis_index("rows"), 2)
    for block in range(n_rows):
        part = whole[block * size : (block + 1) * size]
        place = pl.ds(block // 2 * size, size)

        @pl.when(core == block % 2)
        def _():
            keep[place, :] = part

        @pl.when(core != block % 2)
        def _():
            send[place, :] = part

    keep[pl.ds(CBLK // 2, TAIL), :] = square
    send[pl.ds(CBLK // 2, TAIL), :] = square


def first_adjoint(n_rows, n_cols, pick, counts, cells, *rest):
    parts, pieces, (u_out, keep, send, table, sums) = rest[:PARTS], rest[PARTS:-5], rest[-5:]
    me = lax.axis_index("cols")
    offset = 0
    for piece in pieces:
        rows = PBLK // n_cols
        for at in range(piece.shape[0] // rows):
            owner = jnp.bitwise_xor(me, offset)
            u_out[pl.ds(pl.multiple_of(owner * rows, rows), rows), :] = piece[pl.ds(at * rows, rows), :]
            offset += 1
    adjoint_tail(n_rows, parts, pick, cells, counts, u_out[...], keep, send, table, sums)


def next_adjoint(last, n_rows, pick, counts, cells, *rest):
    parts = rest[:PARTS]
    mine, other, u_old, beta_old, *rest = rest[PARTS:]
    u_out = None if last else rest.pop(0)
    alpha_out, keep, send, table, sums = rest
    total = mine[...] + other[...]
    alpha = jnp.sqrt(total[PBLK:])
    alpha_out[...] = alpha
    u = total[:PBLK] / alpha[:1] - alpha[:1] * (u_old[...] / beta_old[:1])
    if not last:
        u_out[...] = u
    adjoint_tail(n_rows, parts, pick, cells, counts, u, keep, send, table, sums)


def cell_vector(n_rows, mine, other, v_old, alpha_old, v_out, beta_out, own_out):
    size, _ = halves(n_rows, CBLK)
    me = lax.axis_index("rows")
    core = lax.rem(me, 2)
    beta = jnp.sqrt(mine[pl.ds(CBLK // 2, TAIL), :])
    beta_out[...] = beta
    for block in range(n_rows):
        place = pl.ds(block // 2 * size, size)
        part = jnp.where(core == block % 2, mine[place, :], other[place, :]) / beta[:1]
        here = pl.ds(block * size, size)
        if v_old is not None:
            part = part - beta[:1] * (v_old[here, :] / alpha_old[:1])
        v_out[here, :] = part
    own_out[...] = v_out[pl.ds(pl.multiple_of(me * size, size), size), :]
    v = v_out[...]
    return v, jnp.full((TAIL, B), jnp.sum(v * v))


def forward(first, n_rows, cell, counts, picks, *rest):
    parts, rest = rest[:PARTS], rest[PARTS:]
    old = (None, None) if first else rest[2:4]
    v_out, beta_out, own_out, out, table, sums = rest[-6:]
    v, square = cell_vector(n_rows, rest[0], rest[1], *old, v_out, beta_out, own_out)
    fill_table(table, v)
    out[:PBLK, :] = over_tiles(parts, counts[0, 0], table, cell, picks, PBLK, sums, PARTS - TURNED)
    out[pl.ds(PBLK, TAIL), :] = square


def last_vector(n_rows, mine, other, v_old, alpha_old, beta_out, own_out, square_out, v):
    _, square_out[...] = cell_vector(n_rows, mine, other, v_old, alpha_old, v, beta_out, own_out)


def finish(*refs):
    blocks, refs = refs[: ITERS + 1], refs[ITERS + 1 :]
    betas, refs = refs[: ITERS + 1], refs[ITERS + 1 :]
    alphas, refs = refs[:ITERS], refs[ITERS:]
    squares, (model_out, search_out) = refs[:-2], refs[-2:]
    betas = [ref[:1] for ref in betas]
    alphas = [ref[:1] for ref in alphas] + [jnp.sqrt(sum(ref[:1] for ref in squares))]
    phibar, rhobar = betas[0], alphas[0]
    search = blocks[0][...] / alphas[0]
    model = jnp.zeros_like(search)
    for step in range(ITERS):
        beta, alpha = betas[step + 1], alphas[step + 1]
        rho = jnp.sqrt(rhobar * rhobar + beta * beta)
        cosine = rhobar / rho
        sine = beta / rho
        theta = sine * alpha
        rhobar = -cosine * alpha
        phi = cosine * phibar
        phibar = sine * phibar
        model = model + phi / rho * search
        search = blocks[step + 1][...] / alpha - theta / rho * search
    model_out[...] = model
    search_out[...] = search


def swapped(block, axis, size, bit):
    return lax.ppermute(block, axis, [(i, i ^ bit) for i in range(size)])


def shape(*dims):
    return jax.ShapeDtypeStruct(dims, jnp.float32)


VECTOR = pl.BlockSpec(memory_space=pltpu.VMEM)
SCALAR = pl.BlockSpec(memory_space=pltpu.SMEM)


def call(kernel, outs, blocks, source, counts, targets, tiles, arrays):
    slots = targets.shape[1]
    return pl.pallas_call(
        kernel,
        out_shape=outs,
        in_specs=[SCALAR] * 2 + [VECTOR] * (1 + len(tiles) + len(arrays)),
        out_specs=[VECTOR] * len(outs),
        scratch_shapes=[
            pltpu.VMEM((2, blocks, B), jnp.float32),
            pltpu.VMEM((slots, B), jnp.float32),
        ],
        compiler_params=pltpu.CompilerParams(vmem_limit_bytes=12 << 20),
    )(source, counts, targets, *tiles, *arrays)


def split_part(kernels, data, start, size):
    passes = data is not None
    if start == 0 and passes:
        data = pltpu.with_memory_space_constraint(data, pltpu.HBM)
    out = pl.pallas_call(
        functools.partial(split_tiles, start, passes),
        out_shape=[pltpu.VMEM((size, 2 * B, B), jnp.bfloat16)]
        + ([shape(*data.shape)] if passes else []),
        in_specs=[pl.BlockSpec(memory_space=pltpu.HBM)] + [pl.BlockSpec(memory_space=pl.ANY)] * passes,
        out_specs=[VECTOR] * (1 + passes),
        scratch_shapes=[
            pltpu.VMEM((BUFFERS, STEP, B, B), jnp.float32),
            pltpu.SemaphoreType.DMA((BUFFERS,)),
        ]
        + [pltpu.SemaphoreType.DMA] * passes,
        cost_estimate=pl.CostEstimate(
            flops=4 * size * B * B, bytes_accessed=4 * size * B * B, transcendentals=0
        ),
        compiler_params=pltpu.CompilerParams(vmem_limit_bytes=12 << 20),
    )(*([kernels, data] if passes else [kernels]))
    return out if passes else (out[0], None)


def turned(tiles, data):
    total = sum(part.shape[0] for part in tiles)
    data, *out = pl.pallas_call(
        turn_tiles,
        out_shape=[shape(*data.shape)] + [pltpu.VMEM(part.shape, part.dtype) for part in tiles],
        in_specs=[VECTOR] * TURNED + [pl.BlockSpec(memory_space=pl.ANY)],
        out_specs=[VECTOR] * (TURNED + 1),
        scratch_shapes=[pltpu.SemaphoreType.DMA],
        cost_estimate=pl.CostEstimate(
            flops=0, bytes_accessed=2 * total * B * B, transcendentals=0
        ),
        compiler_params=pltpu.CompilerParams(vmem_limit_bytes=4 << 20),
    )(*tiles, data)
    return data, out


def simple_call(kernel, outs, arrays, scratch=()):
    return pl.pallas_call(
        kernel,
        out_shape=outs,
        in_specs=[VECTOR] * len(arrays),
        out_specs=[VECTOR] * len(outs),
        scratch_shapes=scratch,
        compiler_params=pltpu.CompilerParams(vmem_limit_bytes=4 << 20),
    )(*arrays)


def per_device(n_rows, n_cols, kernels, pick_index, cell_index, counts, data):
    slots = kernels.shape[0]
    by_pick = (pick_index, counts, cell_index.reshape(1, slots))
    by_cell = (cell_index, counts, pick_index.reshape(1, slots))
    half = CBLK // 2 + TAIL
    own = CBLK // n_rows

    transposed = []

    def sum_cells(keep, send):
        mine = keep + swapped(send, "rows", n_rows, 1)
        bit = 2
        while bit < n_rows:
            other = swapped(mine, "rows", n_rows, bit)
            if not transposed:
                mine, parts = turned(tiles[:TURNED], mine)
                transposed.extend(parts + tiles[TURNED:])
            mine = mine + other
            bit *= 2
        return [mine, swapped(mine, "rows", n_rows, 1)]

    kernels = pltpu.with_memory_space_constraint(kernels, pltpu.HBM)
    tiles = []
    held = data
    partner = None
    bit = 1
    for share in SHARES:
        if bit < n_cols:
            held = held if partner is None else jnp.concatenate([held, partner], axis=0)
            partner = swapped(held, "cols", n_cols, bit)
            bit *= 2
        start = sum(part.shape[0] for part in tiles)
        more = bit < n_cols
        part, passed = split_part(
            kernels, held if more else None, start, slots * share // sum(SHARES)
        )
        tiles.append(part)
        if more:
            held = passed
    while bit < n_cols:
        held = jnp.concatenate([held, partner], axis=0)
        partner = swapped(held, "cols", n_cols, bit)
        bit *= 2
    pieces = [held, partner]
    upick, keep, send = call(
        functools.partial(first_adjoint, n_rows, n_cols),
        [shape(PBLK, B), shape(half, B), shape(half, B)],
        PBLK,
        *by_pick,
        tiles,
        pieces,
    )
    old = []
    blocks, alphas, betas = [], [], []
    for step in range(ITERS):
        sums = sum_cells(keep, send)
        vcell, beta, block, product = call(
            functools.partial(forward, step == 0, n_rows),
            [shape(CBLK, B), shape(TAIL, B), shape(own, B), shape(PBLK + TAIL, B)],
            CBLK,
            *by_cell,
            transposed,
            sums + old,
        )
        blocks.append(block)
        betas.append(beta)
        bit = 1
        while 2 * bit < n_cols:
            product = product + swapped(product, "cols", n_cols, bit)
            bit *= 2
        last = step == ITERS - 1
        *passed, alpha, keep, send = call(
            functools.partial(next_adjoint, last, n_rows),
            [shape(PBLK, B)] * (not last) + [shape(TAIL, B), shape(half, B), shape(half, B)],
            PBLK,
            *by_pick,
            tiles,
            [product, swapped(product, "cols", n_cols, bit), upick, beta],
        )
        upick = passed[0] if passed else None
        alphas.append(alpha)
        old = [vcell, alpha]
    beta, block, square = simple_call(
        functools.partial(last_vector, n_rows),
        [shape(TAIL, B), shape(own, B), shape(TAIL, B)],
        sum_cells(keep, send) + old,
        [pltpu.VMEM((CBLK, B), jnp.float32)],
    )
    blocks.append(block)
    betas.append(beta)
    square = square + swapped(square, "cols", n_cols, 1)
    squares = [square] + [swapped(square, "cols", n_cols, bit) for bit in range(2, n_cols, 2)]
    model, search = simple_call(
        finish, [shape(own, B), shape(own, B)], blocks + betas + alphas + squares
    )
    return (model, search)


def solution(mesh):
    def run(*args):
        return per_device(mesh.shape["rows"], mesh.shape["cols"], *args)

    return jax.shard_map(
        run,
        mesh=mesh,
        in_specs=(
            P(("rows", "cols"), None, None),
            P(("rows", "cols")),
            P(("rows", "cols")),
            P("rows", "cols"),
            P("cols", "rows"),
        ),
        out_specs=(P("rows", "cols"), P("rows", "cols")),
        check_vma=False,
    )
```

```python
import functools

import jax
import jax.numpy as jnp
from jax import lax
from jax.experimental import pallas as pl
from jax.experimental.pallas import tpu as pltpu
from jax.sharding import PartitionSpec as P

PBLK = 128
CBLK = 512
ITERS = 2
B = 128
SUB = 8
GROUP = 80
PARTS = 2
TURNED = 1
STEP = 8
BUFFERS = 8
CHUNK = 32
TAIL = 8


def split(value):
    high = value.astype(jnp.bfloat16)
    return high, (value - high.astype(jnp.float32)).astype(jnp.bfloat16)


def split_tiles(start, passes, tiles, *rest):
    if passes:
        data, out, data_out, held, arrived, passed = rest
        through = pltpu.make_async_copy(data, data_out, passed)
        through.start()
    else:
        out, held, arrived = rest
    steps = out.shape[0] // STEP

    def copy(step):
        slot = lax.rem(step, BUFFERS)
        return pltpu.make_async_copy(
            tiles.at[pl.ds(start + step * STEP, STEP)], held.at[slot], arrived.at[slot]
        )

    for step in range(min(BUFFERS - 1, steps)):
        copy(jnp.int32(step)).start()

    def one(step, carry):
        @pl.when(step + BUFFERS - 1 < steps)
        def _():
            copy(step + BUFFERS - 1).start()

        copy(step).wait()
        slot = lax.rem(step, BUFFERS)
        for k in range(STEP):
            for row in range(0, B, CHUNK):
                high, low = split(held[slot, k, pl.ds(row, CHUNK), :])
                out[step * STEP + k, pl.ds(row, CHUNK), :] = high
                out[step * STEP + k, pl.ds(B + row, CHUNK), :] = low
        return carry

    lax.fori_loop(0, steps, one, 0)
    if passes:
        through.wait()


def turn_tiles(*refs):
    through = pltpu.make_async_copy(refs[TURNED], refs[TURNED + 1], refs[-1])
    through.start()
    for tiles, out in zip(refs[:TURNED], refs[TURNED + 2 : -1]):

        def one(k, carry, tiles=tiles, out=out):
            out[k, :B, :] = tiles[k, :B, :].T
            out[k, B:, :] = tiles[k, B:, :].T
            return carry

        lax.fori_loop(0, tiles.shape[0], one, 0, unroll=8)
    through.wait()


def fill_table(table, value):
    for index, term in enumerate(split(value)):
        table[index] = term.astype(jnp.float32)


def row_pair(table, source, slot, at, turned):
    place = lax.broadcasted_iota(jnp.int32, (SUB, B), 0)

    def term(n, index):
        row = jnp.broadcast_to(table[index, pl.ds(source[slot + n], 1), :], (SUB, B))
        return jnp.where(place == at + n, row, 0.0)

    def both(*tiles):
        terms = [sum(term(n, index) for n in tiles) for index in range(2)]
        return jnp.concatenate(terms, axis=0).astype(jnp.bfloat16)

    if turned:
        return jnp.concatenate([both(0), both(1)], axis=1)
    return jnp.concatenate([both(0, 1)] * 2, axis=1)


def eight(tiles, base, table, source, slot, turned):
    total = jnp.zeros((2 * SUB, 2 * B), jnp.float32)
    over = ((1,), (1 if turned else 0,))
    for k in range(0, SUB, 2):
        pair = jnp.concatenate([tiles[base + k], tiles[base + k + 1]], axis=1)
        row = row_pair(table, source, slot + k, k, turned)
        total += lax.dot_general(row, pair, (over, ((), ())), preferred_element_type=jnp.float32)
    total = total[:SUB] + total[SUB:]
    if turned:
        return total[:, :B] + total[:, B:]
    odd = lax.rem(lax.broadcasted_iota(jnp.int32, (SUB, B), 0), 2) == 1
    return jnp.where(odd, total[:, B:], total[:, :B])


def over_tiles(parts, live, table, source, targets, blocks, sums, turned=0):
    sums[...] = jnp.zeros_like(sums)
    first = 0
    for part, tiles in enumerate(parts):
        size = tiles.shape[0]
        turn = part >= len(parts) - turned
        here = jnp.clip(live - first, 0, size)

        def some(group, carry, tiles=tiles, first=first, turn=turn):
            for k in range(0, GROUP, SUB):
                base = group * GROUP + k
                slot = first + base
                value = eight(tiles, base, table, source, slot, turn)
                sums[pl.ds(pl.multiple_of(slot, SUB), SUB), :] = value
            return carry

        lax.fori_loop(0, (here + GROUP - 1) // GROUP, some, 0)
        first += size
    slots = sums.shape[0]
    block = lax.broadcasted_iota(jnp.int32, (blocks, slots), 0)
    slot = lax.broadcasted_iota(jnp.int32, (1, slots), 1)
    chosen = block == jnp.where(slot < live, targets[...], -1)
    chosen = jnp.where(chosen, 1.0, 0.0).astype(jnp.bfloat16)
    both = jnp.concatenate(split(sums[...]), axis=1)
    total = jnp.dot(chosen, both, preferred_element_type=jnp.float32)
    return total[:, :B] + total[:, B:]


def halves(n_rows, cells):
    size = cells // n_rows
    return size, [range(core, n_rows, 2) for core in range(2)]


def adjoint_tail(n_rows, parts, pick, cells, counts, u, keep, send, table, sums):
    fill_table(table, u)
    whole = over_tiles(parts, counts[0, 0], table, pick, cells, CBLK, sums)
    square = jnp.full((TAIL, B), jnp.sum(u * u))
    size, _ = halves(n_rows, CBLK)
    core = lax.rem(lax.axis_index("rows"), 2)
    for block in range(n_rows):
        part = whole[block * size : (block + 1) * size]
        place = pl.ds(block // 2 * size, size)

        @pl.when(core == block % 2)
        def _():
            keep[place, :] = part

        @pl.when(core != block % 2)
        def _():
            send[place, :] = part

    keep[pl.ds(CBLK // 2, TAIL), :] = square
    send[pl.ds(CBLK // 2, TAIL), :] = square


def first_adjoint(n_rows, n_cols, pick, counts, cells, *rest):
    parts, pieces, (u_out, keep, send, table, sums) = rest[:PARTS], rest[PARTS:-5], rest[-5:]
    me = lax.axis_index("cols")
    offset = 0
    for piece in pieces:
        rows = PBLK // n_cols
        for at in range(piece.shape[0] // rows):
            owner = jnp.bitwise_xor(me, offset)
            u_out[pl.ds(pl.multiple_of(owner * rows, rows), rows), :] = piece[pl.ds(at * rows, rows), :]
            offset += 1
    adjoint_tail(n_rows, parts, pick, cells, counts, u_out[...], keep, send, table, sums)


def next_adjoint(last, n_rows, pick, counts, cells, *rest):
    parts = rest[:PARTS]
    mine, other, u_old, beta_old, *rest = rest[PARTS:]
    u_out = None if last else rest.pop(0)
    alpha_out, keep, send, table, sums = rest
    total = mine[...] + other[...]
    alpha = jnp.sqrt(total[PBLK:])
    alpha_out[...] = alpha
    u = total[:PBLK] / alpha[:1] - alpha[:1] * (u_old[...] / beta_old[:1])
    if not last:
        u_out[...] = u
    adjoint_tail(n_rows, parts, pick, cells, counts, u, keep, send, table, sums)


def cell_vector(n_rows, mine, other, v_old, alpha_old, v_out, beta_out, own_out):
    size, _ = halves(n_rows, CBLK)
    me = lax.axis_index("rows")
    core = lax.rem(me, 2)
    beta = jnp.sqrt(mine[pl.ds(CBLK // 2, TAIL), :])
    beta_out[...] = beta
    for block in range(n_rows):
        place = pl.ds(block // 2 * size, size)
        part = jnp.where(core == block % 2, mine[place, :], other[place, :]) / beta[:1]
        here = pl.ds(block * size, size)
        if v_old is not None:
            part = part - beta[:1] * (v_old[here, :] / alpha_old[:1])
        v_out[here, :] = part
    own_out[...] = v_out[pl.ds(pl.multiple_of(me * size, size), size), :]
    v = v_out[...]
    return v, jnp.full((TAIL, B), jnp.sum(v * v))


def forward(first, n_rows, cell, counts, picks, *rest):
    parts, rest = rest[:PARTS], rest[PARTS:]
    old = (None, None) if first else rest[2:4]
    v_out, beta_out, own_out, out, table, sums = rest[-6:]
    v, square = cell_vector(n_rows, rest[0], rest[1], *old, v_out, beta_out, own_out)
    fill_table(table, v)
    out[:PBLK, :] = over_tiles(parts, counts[0, 0], table, cell, picks, PBLK, sums, PARTS - TURNED)
    out[pl.ds(PBLK, TAIL), :] = square


def last_vector(n_rows, mine, v_old, alpha_old, beta_out, own_out, square_out, v):
    size, _ = halves(n_rows, CBLK)
    me = lax.axis_index("rows")
    beta = jnp.sqrt(mine[pl.ds(CBLK // 2, TAIL), :])
    beta_out[...] = beta
    for block in range(n_rows // 2):
        here = pl.ds(block * size, size)
        whole = pl.ds(pl.multiple_of((2 * block + lax.rem(me, 2)) * size, size), size)
        v[here, :] = mine[here, :] / beta[:1] - beta[:1] * (v_old[whole, :] / alpha_old[:1])
    own_out[...] = v[pl.ds(pl.multiple_of(lax.div(me, 2) * size, size), size), :]
    half = v[...]
    square_out[...] = jnp.full((TAIL, B), jnp.sum(half * half))


def finish(*refs):
    blocks, refs = refs[: ITERS + 1], refs[ITERS + 1 :]
    betas, refs = refs[: ITERS + 1], refs[ITERS + 1 :]
    alphas, refs = refs[:ITERS], refs[ITERS:]
    squares, (model_out, search_out) = refs[:-2], refs[-2:]
    betas = [ref[:1] for ref in betas]
    alphas = [ref[:1] for ref in alphas] + [jnp.sqrt(sum(ref[:1] for ref in squares))]
    phibar, rhobar = betas[0], alphas[0]
    search = blocks[0][...] / alphas[0]
    model = jnp.zeros_like(search)
    for step in range(ITERS):
        beta, alpha = betas[step + 1], alphas[step + 1]
        rho = jnp.sqrt(rhobar * rhobar + beta * beta)
        cosine = rhobar / rho
        sine = beta / rho
        theta = sine * alpha
        rhobar = -cosine * alpha
        phi = cosine * phibar
        phibar = sine * phibar
        model = model + phi / rho * search
        search = blocks[step + 1][...] / alpha - theta / rho * search
    model_out[...] = model
    search_out[...] = search


def swapped(block, axis, size, bit):
    return lax.ppermute(block, axis, [(i, i ^ bit) for i in range(size)])


def shape(*dims):
    return jax.ShapeDtypeStruct(dims, jnp.float32)


VECTOR = pl.BlockSpec(memory_space=pltpu.VMEM)
SCALAR = pl.BlockSpec(memory_space=pltpu.SMEM)


def call(kernel, outs, blocks, source, counts, targets, tiles, arrays):
    slots = targets.shape[1]
    return pl.pallas_call(
        kernel,
        out_shape=outs,
        in_specs=[SCALAR] * 2 + [VECTOR] * (1 + len(tiles) + len(arrays)),
        out_specs=[VECTOR] * len(outs),
        scratch_shapes=[
            pltpu.VMEM((2, blocks, B), jnp.float32),
            pltpu.VMEM((slots, B), jnp.float32),
        ],
        compiler_params=pltpu.CompilerParams(vmem_limit_bytes=12 << 20),
    )(source, counts, targets, *tiles, *arrays)


def split_part(kernels, data, start, size):
    passes = data is not None
    if start == 0 and passes:
        data = pltpu.with_memory_space_constraint(data, pltpu.HBM)
    out = pl.pallas_call(
        functools.partial(split_tiles, start, passes),
        out_shape=[pltpu.VMEM((size, 2 * B, B), jnp.bfloat16)]
        + ([shape(*data.shape)] if passes else []),
        in_specs=[pl.BlockSpec(memory_space=pltpu.HBM)] + [pl.BlockSpec(memory_space=pl.ANY)] * passes,
        out_specs=[VECTOR] * (1 + passes),
        scratch_shapes=[
            pltpu.VMEM((BUFFERS, STEP, B, B), jnp.float32),
            pltpu.SemaphoreType.DMA((BUFFERS,)),
        ]
        + [pltpu.SemaphoreType.DMA] * passes,
        cost_estimate=pl.CostEstimate(
            flops=4 * size * B * B, bytes_accessed=4 * size * B * B, transcendentals=0
        ),
        compiler_params=pltpu.CompilerParams(vmem_limit_bytes=12 << 20),
    )(*([kernels, data] if passes else [kernels]))
    return out if passes else (out[0], None)


def turned(tiles, data):
    total = sum(part.shape[0] for part in tiles)
    data, *out = pl.pallas_call(
        turn_tiles,
        out_shape=[shape(*data.shape)] + [pltpu.VMEM(part.shape, part.dtype) for part in tiles],
        in_specs=[VECTOR] * TURNED + [pl.BlockSpec(memory_space=pl.ANY)],
        out_specs=[VECTOR] * (TURNED + 1),
        scratch_shapes=[pltpu.SemaphoreType.DMA],
        cost_estimate=pl.CostEstimate(
            flops=0, bytes_accessed=2 * total * B * B, transcendentals=0
        ),
        compiler_params=pltpu.CompilerParams(vmem_limit_bytes=4 << 20),
    )(*tiles, data)
    return data, out


def simple_call(kernel, outs, arrays, scratch=()):
    return pl.pallas_call(
        kernel,
        out_shape=outs,
        in_specs=[VECTOR] * len(arrays),
        out_specs=[VECTOR] * len(outs),
        scratch_shapes=scratch,
        compiler_params=pltpu.CompilerParams(vmem_limit_bytes=4 << 20),
    )(*arrays)


def per_device(n_rows, n_cols, kernels, pick_index, cell_index, counts, data):
    slots = kernels.shape[0]
    by_pick = (pick_index, counts, cell_index.reshape(1, slots))
    by_cell = (cell_index, counts, pick_index.reshape(1, slots))
    half = CBLK // 2 + TAIL
    own = CBLK // n_rows

    transposed = []

    def sum_half(keep, send):
        mine = keep + swapped(send, "rows", n_rows, 1)
        bit = 2
        while bit < n_rows:
            other = swapped(mine, "rows", n_rows, bit)
            if not transposed:
                mine, parts = turned(tiles[:TURNED], mine)
                transposed.extend(parts + tiles[TURNED:])
            mine = mine + other
            bit *= 2
        return mine

    def sum_cells(keep, send):
        mine = sum_half(keep, send)
        return [mine, swapped(mine, "rows", n_rows, 1)]

    kernels = pltpu.with_memory_space_constraint(kernels, pltpu.HBM)
    half_slots = slots // 2
    partner = swapped(data, "cols", n_cols, 1)
    first, passed = split_part(kernels, data, 0, half_slots)
    second, _ = split_part(kernels, None, half_slots, slots - half_slots)
    tiles = [first, second]
    pair = jnp.concatenate([passed, partner], axis=0)
    pieces = [pair] + [swapped(pair, "cols", n_cols, bit) for bit in range(2, n_cols, 2)]
    upick, keep, send = call(
        functools.partial(first_adjoint, n_rows, n_cols),
        [shape(PBLK, B), shape(half, B), shape(half, B)],
        PBLK,
        *by_pick,
        tiles,
        pieces,
    )
    old = []
    blocks, alphas, betas = [], [], []
    for step in range(ITERS):
        sums = sum_cells(keep, send)
        vcell, beta, block, product = call(
            functools.partial(forward, step == 0, n_rows),
            [shape(CBLK, B), shape(TAIL, B), shape(own, B), shape(PBLK + TAIL, B)],
            CBLK,
            *by_cell,
            transposed,
            sums + old,
        )
        blocks.append(block)
        betas.append(beta)
        bit = 1
        while 2 * bit < n_cols:
            product = product + swapped(product, "cols", n_cols, bit)
            bit *= 2
        last = step == ITERS - 1
        *passed, alpha, keep, send = call(
            functools.partial(next_adjoint, last, n_rows),
            [shape(PBLK, B)] * (not last) + [shape(TAIL, B), shape(half, B), shape(half, B)],
            PBLK,
            *by_pick,
            tiles,
            [product, swapped(product, "cols", n_cols, bit), upick, beta],
        )
        upick = passed[0] if passed else None
        alphas.append(alpha)
        old = [vcell, alpha]
    beta, block, square = simple_call(
        functools.partial(last_vector, n_rows),
        [shape(TAIL, B), shape(own, B), shape(TAIL, B)],
        [sum_half(keep, send)] + old,
        [pltpu.VMEM((CBLK // 2, B), jnp.float32)],
    )
    blocks.append(block)
    betas.append(beta)
    both = [
        (r * n_cols + c, (r ^ 1) * n_cols + (c ^ 1)) for r in range(n_rows) for c in range(n_cols)
    ]
    square = (square + swapped(square, "rows", n_rows, 1)) + (
        swapped(square, "cols", n_cols, 1) + lax.ppermute(square, ("rows", "cols"), both)
    )
    squares = [square] + [swapped(square, "cols", n_cols, bit) for bit in range(2, n_cols, 2)]
    model, search = simple_call(
        finish, [shape(own, B), shape(own, B)], blocks + betas + alphas + squares
    )
    return (model, search)


def solution(mesh):
    def run(*args):
        return per_device(mesh.shape["rows"], mesh.shape["cols"], *args)

    return jax.shard_map(
        run,
        mesh=mesh,
        in_specs=(
            P(("rows", "cols"), None, None),
            P(("rows", "cols")),
            P(("rows", "cols")),
            P("rows", "cols"),
            P("cols", "rows"),
        ),
        out_specs=(P("rows", "cols"), P("rows", "cols")),
        check_vma=False,
    )
```

```python
import functools

import jax
import jax.numpy as jnp
from jax import lax
from jax.experimental import pallas as pl
from jax.experimental.pallas import tpu as pltpu
from jax.sharding import PartitionSpec as P

PBLK = 128
CBLK = 512
ITERS = 2
B = 128
SUB = 8
GROUP = 160
PARTS = 2
TURNED = 1
STEP = 8
BUFFERS = 8
CHUNK = 32
TAIL = 8


def split(value):
    high = value.astype(jnp.bfloat16)
    return high, (value - high.astype(jnp.float32)).astype(jnp.bfloat16)


def split_tiles(start, passes, tiles, *rest):
    if passes:
        data, out, data_out, held, arrived, passed = rest
        through = pltpu.make_async_copy(data, data_out, passed)
        through.start()
    else:
        out, held, arrived = rest
    steps = out.shape[0] // STEP

    def copy(step):
        slot = lax.rem(step, BUFFERS)
        return pltpu.make_async_copy(
            tiles.at[pl.ds(start + step * STEP, STEP)], held.at[slot], arrived.at[slot]
        )

    for step in range(min(BUFFERS - 1, steps)):
        copy(jnp.int32(step)).start()

    def one(step, carry):
        @pl.when(step + BUFFERS - 1 < steps)
        def _():
            copy(step + BUFFERS - 1).start()

        copy(step).wait()
        slot = lax.rem(step, BUFFERS)
        for k in range(STEP):
            for row in range(0, B, CHUNK):
                high, low = split(held[slot, k, pl.ds(row, CHUNK), :])
                out[step * STEP + k, pl.ds(row, CHUNK), :] = high
                out[step * STEP + k, pl.ds(B + row, CHUNK), :] = low
        return carry

    lax.fori_loop(0, steps, one, 0)
    if passes:
        through.wait()


def turn_tiles(*refs):
    through = pltpu.make_async_copy(refs[TURNED], refs[TURNED + 1], refs[-1])
    through.start()
    for tiles, out in zip(refs[:TURNED], refs[TURNED + 2 : -1]):

        def one(k, carry, tiles=tiles, out=out):
            out[k, :B, :] = tiles[k, :B, :].T
            out[k, B:, :] = tiles[k, B:, :].T
            return carry

        lax.fori_loop(0, tiles.shape[0], one, 0, unroll=8)
    through.wait()


def fill_table(table, value):
    for index, term in enumerate(split(value)):
        table[index] = term.astype(jnp.float32)


def row_pair(table, source, slot, at, turned):
    place = lax.broadcasted_iota(jnp.int32, (SUB, B), 0)

    def term(n, index):
        row = jnp.broadcast_to(table[index, pl.ds(source[slot + n], 1), :], (SUB, B))
        return jnp.where(place == at + n, row, 0.0)

    def both(*tiles):
        terms = [sum(term(n, index) for n in tiles) for index in range(2)]
        return jnp.concatenate(terms, axis=0).astype(jnp.bfloat16)

    if turned:
        return jnp.concatenate([both(0), both(1)], axis=1)
    return jnp.concatenate([both(0, 1)] * 2, axis=1)


def eight(tiles, base, table, source, slot, turned):
    total = jnp.zeros((2 * SUB, 2 * B), jnp.float32)
    over = ((1,), (1 if turned else 0,))
    for k in range(0, SUB, 2):
        pair = jnp.concatenate([tiles[base + k], tiles[base + k + 1]], axis=1)
        row = row_pair(table, source, slot + k, k, turned)
        total += lax.dot_general(row, pair, (over, ((), ())), preferred_element_type=jnp.float32)
    total = total[:SUB] + total[SUB:]
    if turned:
        return total[:, :B] + total[:, B:]
    odd = lax.rem(lax.broadcasted_iota(jnp.int32, (SUB, B), 0), 2) == 1
    return jnp.where(odd, total[:, B:], total[:, :B])


def over_tiles(parts, live, table, source, targets, blocks, sums, turned=0):
    sums[...] = jnp.zeros_like(sums)
    first = 0
    for part, tiles in enumerate(parts):
        size = tiles.shape[0]
        turn = part >= len(parts) - turned
        here = jnp.clip(live - first, 0, size)

        def some(group, carry, tiles=tiles, first=first, turn=turn):
            for k in range(0, GROUP, SUB):
                base = group * GROUP + k
                slot = first + base
                value = eight(tiles, base, table, source, slot, turn)
                sums[pl.ds(pl.multiple_of(slot, SUB), SUB), :] = value
            return carry

        lax.fori_loop(0, (here + GROUP - 1) // GROUP, some, 0)
        first += size
    slots = sums.shape[0]
    block = lax.broadcasted_iota(jnp.int32, (blocks, slots), 0)
    slot = lax.broadcasted_iota(jnp.int32, (1, slots), 1)
    chosen = block == jnp.where(slot < live, targets[...], -1)
    chosen = jnp.where(chosen, 1.0, 0.0).astype(jnp.bfloat16)
    both = jnp.concatenate(split(sums[...]), axis=1)
    total = jnp.dot(chosen, both, preferred_element_type=jnp.float32)
    return total[:, :B] + total[:, B:]


def halves(n_rows, cells):
    size = cells // n_rows
    return size, [range(core, n_rows, 2) for core in range(2)]


def adjoint_tail(n_rows, parts, pick, cells, counts, u, keep, send, table, sums):
    fill_table(table, u)
    whole = over_tiles(parts, counts[0, 0], table, pick, cells, CBLK, sums)
    square = jnp.full((TAIL, B), jnp.sum(u * u))
    size, _ = halves(n_rows, CBLK)
    core = lax.rem(lax.axis_index("rows"), 2)
    for block in range(n_rows):
        part = whole[block * size : (block + 1) * size]
        place = pl.ds(block // 2 * size, size)

        @pl.when(core == block % 2)
        def _():
            keep[place, :] = part

        @pl.when(core != block % 2)
        def _():
            send[place, :] = part

    keep[pl.ds(CBLK // 2, TAIL), :] = square
    send[pl.ds(CBLK // 2, TAIL), :] = square


def first_adjoint(n_rows, n_cols, pick, counts, cells, *rest):
    parts, pieces, (u_out, keep, send, table, sums) = rest[:PARTS], rest[PARTS:-5], rest[-5:]
    me = lax.axis_index("cols")
    offset = 0
    for piece in pieces:
        rows = PBLK // n_cols
        for at in range(piece.shape[0] // rows):
            owner = jnp.bitwise_xor(me, offset)
            u_out[pl.ds(pl.multiple_of(owner * rows, rows), rows), :] = piece[pl.ds(at * rows, rows), :]
            offset += 1
    adjoint_tail(n_rows, parts, pick, cells, counts, u_out[...], keep, send, table, sums)


def next_adjoint(last, n_rows, pick, counts, cells, *rest):
    parts = rest[:PARTS]
    mine, other, u_old, beta_old, *rest = rest[PARTS:]
    u_out = None if last else rest.pop(0)
    alpha_out, keep, send, table, sums = rest
    total = mine[...] + other[...]
    alpha = jnp.sqrt(total[PBLK:])
    alpha_out[...] = alpha
    u = total[:PBLK] / alpha[:1] - alpha[:1] * (u_old[...] / beta_old[:1])
    if not last:
        u_out[...] = u
    adjoint_tail(n_rows, parts, pick, cells, counts, u, keep, send, table, sums)


def cell_vector(n_rows, mine, other, v_old, alpha_old, v_out, beta_out, own_out):
    size, _ = halves(n_rows, CBLK)
    me = lax.axis_index("rows")
    core = lax.rem(me, 2)
    beta = jnp.sqrt(mine[pl.ds(CBLK // 2, TAIL), :])
    beta_out[...] = beta
    for block in range(n_rows):
        place = pl.ds(block // 2 * size, size)
        part = jnp.where(core == block % 2, mine[place, :], other[place, :]) / beta[:1]
        here = pl.ds(block * size, size)
        if v_old is not None:
            part = part - beta[:1] * (v_old[here, :] / alpha_old[:1])
        v_out[here, :] = part
    own_out[...] = v_out[pl.ds(pl.multiple_of(me * size, size), size), :]
    v = v_out[...]
    return v, jnp.full((TAIL, B), jnp.sum(v * v))


def forward(first, n_rows, cell, counts, picks, *rest):
    parts, rest = rest[:PARTS], rest[PARTS:]
    old = (None, None) if first else rest[2:4]
    v_out, beta_out, own_out, out, table, sums = rest[-6:]
    v, square = cell_vector(n_rows, rest[0], rest[1], *old, v_out, beta_out, own_out)
    fill_table(table, v)
    out[:PBLK, :] = over_tiles(parts, counts[0, 0], table, cell, picks, PBLK, sums, PARTS - TURNED)
    out[pl.ds(PBLK, TAIL), :] = square


def last_vector(n_rows, mine, v_old, alpha_old, beta_out, own_out, square_out, v):
    size, _ = halves(n_rows, CBLK)
    me = lax.axis_index("rows")
    beta = jnp.sqrt(mine[pl.ds(CBLK // 2, TAIL), :])
    beta_out[...] = beta
    for block in range(n_rows // 2):
        here = pl.ds(block * size, size)
        whole = pl.ds(pl.multiple_of((2 * block + lax.rem(me, 2)) * size, size), size)
        v[here, :] = mine[here, :] / beta[:1] - beta[:1] * (v_old[whole, :] / alpha_old[:1])
    own_out[...] = v[pl.ds(pl.multiple_of(lax.div(me, 2) * size, size), size), :]
    half = v[...]
    square_out[...] = jnp.full((TAIL, B), jnp.sum(half * half))


def finish(*refs):
    blocks, refs = refs[: ITERS + 1], refs[ITERS + 1 :]
    betas, refs = refs[: ITERS + 1], refs[ITERS + 1 :]
    alphas, refs = refs[:ITERS], refs[ITERS:]
    squares, (model_out, search_out) = refs[:-2], refs[-2:]
    betas = [ref[:1] for ref in betas]
    alphas = [ref[:1] for ref in alphas] + [jnp.sqrt(sum(ref[:1] for ref in squares))]
    phibar, rhobar = betas[0], alphas[0]
    search = blocks[0][...] / alphas[0]
    model = jnp.zeros_like(search)
    for step in range(ITERS):
        beta, alpha = betas[step + 1], alphas[step + 1]
        rho = jnp.sqrt(rhobar * rhobar + beta * beta)
        cosine = rhobar / rho
        sine = beta / rho
        theta = sine * alpha
        rhobar = -cosine * alpha
        phi = cosine * phibar
        phibar = sine * phibar
        model = model + phi / rho * search
        search = blocks[step + 1][...] / alpha - theta / rho * search
    model_out[...] = model
    search_out[...] = search


def swapped(block, axis, size, bit):
    return lax.ppermute(block, axis, [(i, i ^ bit) for i in range(size)])


def shape(*dims):
    return jax.ShapeDtypeStruct(dims, jnp.float32)


VECTOR = pl.BlockSpec(memory_space=pltpu.VMEM)
SCALAR = pl.BlockSpec(memory_space=pltpu.SMEM)


def call(kernel, outs, blocks, source, counts, targets, tiles, arrays):
    slots = targets.shape[1]
    return pl.pallas_call(
        kernel,
        out_shape=outs,
        in_specs=[SCALAR] * 2 + [VECTOR] * (1 + len(tiles) + len(arrays)),
        out_specs=[VECTOR] * len(outs),
        scratch_shapes=[
            pltpu.VMEM((2, blocks, B), jnp.float32),
            pltpu.VMEM((slots, B), jnp.float32),
        ],
        compiler_params=pltpu.CompilerParams(vmem_limit_bytes=12 << 20),
    )(source, counts, targets, *tiles, *arrays)


def split_part(kernels, data, start, size):
    passes = data is not None
    if start == 0 and passes:
        data = pltpu.with_memory_space_constraint(data, pltpu.HBM)
    out = pl.pallas_call(
        functools.partial(split_tiles, start, passes),
        out_shape=[pltpu.VMEM((size, 2 * B, B), jnp.bfloat16)]
        + ([shape(*data.shape)] if passes else []),
        in_specs=[pl.BlockSpec(memory_space=pltpu.HBM)] + [pl.BlockSpec(memory_space=pl.ANY)] * passes,
        out_specs=[VECTOR] * (1 + passes),
        scratch_shapes=[
            pltpu.VMEM((BUFFERS, STEP, B, B), jnp.float32),
            pltpu.SemaphoreType.DMA((BUFFERS,)),
        ]
        + [pltpu.SemaphoreType.DMA] * passes,
        cost_estimate=pl.CostEstimate(
            flops=4 * size * B * B, bytes_accessed=4 * size * B * B, transcendentals=0
        ),
        compiler_params=pltpu.CompilerParams(vmem_limit_bytes=12 << 20),
    )(*([kernels, data] if passes else [kernels]))
    return out if passes else (out[0], None)


def turned(tiles, data):
    total = sum(part.shape[0] for part in tiles)
    data, *out = pl.pallas_call(
        turn_tiles,
        out_shape=[shape(*data.shape)] + [pltpu.VMEM(part.shape, part.dtype) for part in tiles],
        in_specs=[VECTOR] * TURNED + [pl.BlockSpec(memory_space=pl.ANY)],
        out_specs=[VECTOR] * (TURNED + 1),
        scratch_shapes=[pltpu.SemaphoreType.DMA],
        cost_estimate=pl.CostEstimate(
            flops=0, bytes_accessed=2 * total * B * B, transcendentals=0
        ),
        compiler_params=pltpu.CompilerParams(vmem_limit_bytes=4 << 20),
    )(*tiles, data)
    return data, out


def simple_call(kernel, outs, arrays, scratch=()):
    return pl.pallas_call(
        kernel,
        out_shape=outs,
        in_specs=[VECTOR] * len(arrays),
        out_specs=[VECTOR] * len(outs),
        scratch_shapes=scratch,
        compiler_params=pltpu.CompilerParams(vmem_limit_bytes=4 << 20),
    )(*arrays)


def per_device(n_rows, n_cols, kernels, pick_index, cell_index, counts, data):
    slots = kernels.shape[0]
    by_pick = (pick_index, counts, cell_index.reshape(1, slots))
    by_cell = (cell_index, counts, pick_index.reshape(1, slots))
    half = CBLK // 2 + TAIL
    own = CBLK // n_rows

    transposed = []

    def sum_half(keep, send):
        mine = keep + swapped(send, "rows", n_rows, 1)
        bit = 2
        while bit < n_rows:
            other = swapped(mine, "rows", n_rows, bit)
            if not transposed:
                mine, parts = turned(tiles[:TURNED], mine)
                transposed.extend(parts + tiles[TURNED:])
            mine = mine + other
            bit *= 2
        return mine

    def sum_cells(keep, send):
        mine = sum_half(keep, send)
        return [mine, swapped(mine, "rows", n_rows, 1)]

    kernels = pltpu.with_memory_space_constraint(kernels, pltpu.HBM)
    half_slots = slots // 2
    partner = swapped(data, "cols", n_cols, 1)
    first, passed = split_part(kernels, data, 0, half_slots)
    second, _ = split_part(kernels, None, half_slots, slots - half_slots)
    tiles = [first, second]
    pair = jnp.concatenate([passed, partner], axis=0)
    pieces = [pair] + [swapped(pair, "cols", n_cols, bit) for bit in range(2, n_cols, 2)]
    upick, keep, send = call(
        functools.partial(first_adjoint, n_rows, n_cols),
        [shape(PBLK, B), shape(half, B), shape(half, B)],
        PBLK,
        *by_pick,
        tiles,
        pieces,
    )
    old = []
    blocks, alphas, betas = [], [], []
    for step in range(ITERS):
        sums = sum_cells(keep, send)
        vcell, beta, block, product = call(
            functools.partial(forward, step == 0, n_rows),
            [shape(CBLK, B), shape(TAIL, B), shape(own, B), shape(PBLK + TAIL, B)],
            CBLK,
            *by_cell,
            transposed,
            sums + old,
        )
        blocks.append(block)
        betas.append(beta)
        bit = 1
        while 2 * bit < n_cols:
            product = product + swapped(product, "cols", n_cols, bit)
            bit *= 2
        last = step == ITERS - 1
        *passed, alpha, keep, send = call(
            functools.partial(next_adjoint, last, n_rows),
            [shape(PBLK, B)] * (not last) + [shape(TAIL, B), shape(half, B), shape(half, B)],
            PBLK,
            *by_pick,
            tiles,
            [product, swapped(product, "cols", n_cols, bit), upick, beta],
        )
        upick = passed[0] if passed else None
        alphas.append(alpha)
        old = [vcell, alpha]
    beta, block, square = simple_call(
        functools.partial(last_vector, n_rows),
        [shape(TAIL, B), shape(own, B), shape(TAIL, B)],
        [sum_half(keep, send)] + old,
        [pltpu.VMEM((CBLK // 2, B), jnp.float32)],
    )
    blocks.append(block)
    betas.append(beta)
    both = [
        (r * n_cols + c, (r ^ 1) * n_cols + (c ^ 1)) for r in range(n_rows) for c in range(n_cols)
    ]
    square = (square + swapped(square, "rows", n_rows, 1)) + (
        swapped(square, "cols", n_cols, 1) + lax.ppermute(square, ("rows", "cols"), both)
    )
    squares = [square] + [swapped(square, "cols", n_cols, bit) for bit in range(2, n_cols, 2)]
    model, search = simple_call(
        finish, [shape(own, B), shape(own, B)], blocks + betas + alphas + squares
    )
    return (model, search)


def solution(mesh):
    def run(*args):
        return per_device(mesh.shape["rows"], mesh.shape["cols"], *args)

    return jax.shard_map(
        run,
        mesh=mesh,
        in_specs=(
            P(("rows", "cols"), None, None),
            P(("rows", "cols")),
            P(("rows", "cols")),
            P("rows", "cols"),
            P("cols", "rows"),
        ),
        out_specs=(P("rows", "cols"), P("rows", "cols")),
        check_vma=False,
    )
```
